128 devices in a mesh: inner: 4 (over y_hi, core), outer: 32 (over z, y_lo, x).
Axes of the slice: x: 4, y: 4 (y_hi: 2, y_lo: 2; y = y_hi * 2 + y_lo), z: 4, core: 2. Of those that a mesh axis runs over, the one named last changes fastest.
Arguments:
- gradients: bfloat16 [128, 4096, 1024], P(('inner', 'outer')), may hold values from -400 to 400
- master: float32 [4096, 1024], P(('inner', 'outer')), may hold values from -0.024 to 0.024
- first_moment: float32 [4096, 1024], P(('inner', 'outer')), may hold values from -0.6 to 0.6
- second_moment: float32 [4096, 1024], P(('inner', 'outer')), may hold values from 0.01 to 0.1
Outputs:
- new_master: float32 [4096, 1024], P(('inner', 'outer'))
- new_first: float32 [4096, 1024], P(('inner', 'outer'))
- new_second: float32 [4096, 1024], P(('inner', 'outer'))
- params: bfloat16 [4096, 1024], replicated
The draws below stay inside these ranges and needn't reach their ends.
All inputs are finite; a program needn't handle non-finite values.
Results may differ from the reference program's by a relative error of at most 0.015.
Values may be sent and summed in bfloat16 or wider, within the bound.
A program may use at most 128 MiB of HBM per device.

```python
import math
import jax
import jax.numpy as jnp
from jax import lax

BLOCK = 1024
BLOCKS = 4096
REPLICAS = 128


def draw_gradients(key, part):
    key = jax.random.fold_in(key, 11)
    subkeys = jax.random.split(key, 4)
    position = jnp.arange(REPLICAS, dtype=jnp.float32) / max(REPLICAS - 1, 1)
    rise = 10.0
    common_weight = 0.05
    overall = 0.4
    shared = jnp.clip(jax.random.normal(subkeys[0], (BLOCKS, BLOCK), jnp.float32), -4.0, 4.0)
    own_part = jnp.clip(jax.random.normal(subkeys[1], (REPLICAS, BLOCKS, BLOCK), jnp.float32), -4.0, 4.0)
    device_scale = jnp.power(rise, position)[:, None, None]
    block_scale = jnp.exp(jax.random.uniform(subkeys[2], (1, BLOCKS, 1), jnp.float32, 0.0, jnp.log(10.0)))
    cell_scale = jnp.exp(jax.random.uniform(subkeys[3], (1, BLOCKS, BLOCK), jnp.float32, 0.0, jnp.log(2.0)))
    values = overall * device_scale * block_scale * cell_scale * (common_weight * shared[None] + own_part)
    return values.astype(jnp.bfloat16)


def steps_of(key, dims, pieces, least, largest):
    loudness, own = 1.0, jax.random.fold_in(key, 6)
    for dim, blocks in pieces:
        steps = jnp.exp(jax.random.uniform(jax.random.fold_in(own, dim), (blocks,), jnp.float32, least / len(pieces), largest / len(pieces)))
        loudness = loudness * jnp.repeat(steps, dims[dim] // blocks).reshape([-1 if axis == dim else 1 for axis in range(len(dims))])
    return loudness


def normal_values(stream_key, dims, deviation, bound, cuts=(), kind=jnp.bfloat16):
    drawn = deviation * jax.random.normal(stream_key, dims, jnp.float32)
    if cuts:
        drawn = drawn * steps_of(stream_key, dims, cuts, -0.22, 0.18)
    return jnp.clip(drawn, -bound, bound).astype(kind)


def setup_inputs(seed: int = 0) -> dict:
    key_of = jax.random.split(jax.random.key(seed), 5)
    return {
        "gradients": draw_gradients(jax.random.fold_in(key_of[4], 71), 0),
        "master": normal_values(key_of[1], (BLOCKS, BLOCK), 0.004, 0.024, ((0, 128),), jnp.float32),
        "first_moment": normal_values(key_of[2], (BLOCKS, BLOCK), 0.1, 0.6, ((0, 128),), jnp.float32),
        "second_moment": jnp.clip(jnp.exp(math.log(0.1) - 2.3025851 * jax.random.uniform(key_of[3], (BLOCKS, BLOCK), jnp.float32) ** steps_of(key_of[3], (BLOCKS, BLOCK), ((0, 128),), -0.2, 0.2)), 0.01, 0.1),
    }


code_levels = 127.0
beta_one = 0.9
beta_two = 0.95
learn_rate = 0.002
decay_rate = 0.1
adam_epsilon = 1e-08
first_fix = 1.0 - 0.9 ** 10
second_fix = 1.0 - 0.95 ** 10

def sign_rows(first_row, row_count, block_width):
    row_ids = first_row + lax.broadcasted_iota(jnp.int32, (row_count, block_width), 0)
    col_ids = lax.broadcasted_iota(jnp.int32, (row_count, block_width), 1)
    hashed = (row_ids * block_width + col_ids) * jnp.int32(-1640531535)
    hashed = jnp.bitwise_xor(hashed, jnp.right_shift(hashed, 15))
    hashed = hashed * jnp.int32(-2048144777)
    return 1 - 2 * jnp.bitwise_and(jnp.right_shift(hashed, 13), 1)

def walsh_rows(values):
    block_width = values.shape[-1]
    leading = values.shape[:-1]
    stride = 1
    while stride < block_width:
        paired = values.reshape(leading + (block_width // (2 * stride), 2, stride))
        upper = paired[..., 0, :]
        lower = paired[..., 1, :]
        values = jnp.stack([upper + lower, upper - lower], axis=-2).reshape(leading + (block_width,))
        stride = stride * 2
    return values

def reference(gradients, master, first_moment, second_moment):
    replicas, blocks, block_width = gradients.shape
    signs = sign_rows(0, blocks, block_width).astype(jnp.float32)
    norm_factor = 1.0 / math.sqrt(block_width)

    def rotate(device_grad):
        return walsh_rows(device_grad.astype(jnp.float32) * signs) * norm_factor
    peaks = lax.map(lambda device_grad: jnp.max(jnp.abs(rotate(device_grad))), gradients)
    global_scale = jnp.max(peaks)
    code_ratio = code_levels / (global_scale + 1e-06)

    def accumulate(running, device_grad):
        codes = jnp.floor(rotate(device_grad) * code_ratio + 0.5).astype(jnp.bfloat16)
        return (running + codes.astype(jnp.float32), None)
    code_sum, _ = lax.scan(accumulate, jnp.zeros((blocks, block_width), jnp.float32), gradients)
    decoded = code_sum * ((global_scale + 1e-06) / (code_levels * replicas))
    mean_grad = signs * (walsh_rows(decoded) * norm_factor)
    new_first = beta_one * first_moment + (1.0 - beta_one) * mean_grad
    new_second = beta_two * second_moment + (1.0 - beta_two) * mean_grad * mean_grad
    step_size = new_first / first_fix / (jnp.sqrt(new_second / second_fix) + adam_epsilon)
    new_master = master - learn_rate * (step_size + decay_rate * master)
    return (new_master, new_first, new_second, new_master.astype(jnp.bfloat16))
```

```python
import functools
import math

import jax
import jax.numpy as jnp
from jax import lax
from jax.experimental import pallas as pl
from jax.experimental.pallas import tpu as pltpu
from jax.sharding import PartitionSpec as P

MESH = pl.DeviceIdType.MESH

code_levels = 127.0
beta_one = 0.9
beta_two = 0.95
learn_rate = 0.002
decay_rate = 0.1
adam_epsilon = 1e-08
first_fix = 1.0 - 0.9**10
second_fix = 1.0 - 0.95**10

blocks = 4096
width = 1024
group = 256
shard = 32
half = 16
lane = 128
tiles = width // lane
units = 2 * tiles
chunk = 256
chunks = blocks // chunk
sub = 128

hash_one = -1640531535
hash_two = ((-2048144777 << 18) & 0xFFFFFFFF) - (1 << 32 if ((-2048144777 << 18) & 0x80000000) else 0)


def wrap(value):
    value &= 0xFFFFFFFF
    return value - (1 << 32) if value & 0x80000000 else value


RS = (0, 2, 4, 6, 8, 10)
AG = (0, 1, 3, 5, 7, 9)


def negative(hashed):
    mixed = jnp.bitwise_xor(hashed, jnp.right_shift(hashed, 15))
    return mixed * jnp.int32(hash_two) < 0


def butterfly(parts):
    p0, p1, p2, p3 = parts
    a, b, c, d = p0 + p1, p0 - p1, p2 + p3, p2 - p3
    return a + c, b + d, a - c, b - d


def pick(order, v0, v1, v2):
    return jnp.where(order == 0, v0, jnp.where(order == 1, v1, v2))


def row_of(axis, v):
    if isinstance(v, int):
        return pick(axis, v * shard, (v % 2) * 128 + (v // 2) * 2048, v * 256)
    return pick(axis, v * shard, lax.rem(v, 2) * 128 + lax.div(v, 2) * 2048, v * 256)


def kernel(
    grad, master, first, second,
    out, new_master, new_first, new_second,
    rot, base, table, peak, peaks, adam_in, total,
    other, core_in, s1, r1, r2, t1, r3, t2, r4, gath, gath_other,
    grad_sem, adam_sem, peak_send, peak_recv,
    rs_send, rs_core, rs_one, rs_two, rs_three, rs_four,
    ag_send, ag_one, ag_two, ag_near, ag_far, ag_core,
):
    inner, outer = lax.axis_index("inner"), lax.axis_index("outer")
    core = lax.rem(inner, 2)
    x = lax.rem(outer, 4)
    y = lax.div(inner, 2) * 2 + lax.rem(lax.div(outer, 4), 2)
    z = lax.div(outer, 8)

    def device(xx, yy, zz, cc):
        return (lax.div(yy, 2) * 2 + cc, zz * 8 + lax.rem(yy, 2) * 4 + xx)

    def step(v, d):
        return lax.rem(v + d, 4)

    near = {}
    for d in (1, 2, 3):
        near[0, d] = device(step(x, d), y, z, core)
        near[1, d] = device(x, step(y, d), z, core)
        near[2, d] = device(x, y, step(z, d), core)
    twin = device(x, y, z, 1 - core)

    def along(axis, d):
        return tuple(pick(axis, near[0, d][n], near[1, d][n], near[2, d][n]) for n in (0, 1))

    def remote(src, dst, send, recv, target):
        return pltpu.make_async_remote_copy(
            src_ref=src, dst_ref=dst, send_sem=send, recv_sem=recv, device_id=target, device_id_type=MESH
        )

    def drain(ref, sem):
        pltpu.make_async_copy(ref, ref, sem).wait()

    barrier = pltpu.get_barrier_semaphore()
    partners = [twin] + [near[axis, d] for axis in (0, 1, 2) for d in (1, 2, 3)]
    for partner in partners:
        pl.semaphore_signal(barrier, inc=1, device_id=partner, device_id_type=MESH)

    def grad_copy(i):
        rows = pl.ds(pl.multiple_of(i * chunk, chunk), chunk)
        return pltpu.make_async_copy(grad.at[0, rows], out.at[rows], grad_sem.at[i])

    def start_grad(i, carry):
        grad_copy(i).start()
        return carry

    lax.fori_loop(0, chunks, start_grad, 0)
    adam_copies = [
        pltpu.make_async_copy(ref, adam_in.at[n], adam_sem.at[n]) for n, ref in enumerate((master, first, second))
    ]
    for copy in adam_copies:
        copy.start()

    rows_i = lax.broadcasted_iota(jnp.int32, (group, group), 0)
    cols_i = lax.broadcasted_iota(jnp.int32, (group, group), 1)
    common = jnp.bitwise_and(rows_i, cols_i)
    for shift in (4, 2, 1):
        common = jnp.bitwise_xor(common, jnp.right_shift(common, shift))
    parity = jnp.bitwise_and(common, 1)
    table[...] = ((1 - 2 * parity).astype(jnp.float32) / math.sqrt(width)).astype(jnp.bfloat16)
    base[...] = (
        lax.broadcasted_iota(jnp.int32, (sub, group), 0) * jnp.int32(wrap(width * hash_one))
        + lax.broadcasted_iota(jnp.int32, (sub, group), 1) * jnp.int32(hash_one)
    )
    peak[...] = jnp.zeros_like(peak)

    def rotate(i, carry):
        @pl.when(lax.rem(i, chunk // sub) == 0)
        def _():
            grad_copy(lax.div(i, chunk // sub)).wait()

        rows = pl.ds(pl.multiple_of(i * sub, sub), sub)
        pieces = []
        for g in range(width // group):
            offset = i * jnp.int32(wrap(sub * width * hash_one)) + jnp.int32(wrap(g * group * hash_one))
            sign = jnp.where(negative(base[...] + offset), -1.0, 1.0).astype(jnp.bfloat16)
            flipped = out[rows, g * group : (g + 1) * group] * sign
            pieces.append(jnp.dot(flipped, table[...], preferred_element_type=jnp.float32))
        top = peak[...]
        for g, piece in enumerate(butterfly(pieces)):
            rot[rows, g * group : (g + 1) * group] = piece
            top = jnp.maximum(top, jnp.max(jnp.abs(piece).reshape(sub // 8, 8, group), axis=0))
        peak[...] = top
        return carry

    lax.fori_loop(0, blocks // sub, rotate, 0)

    pl.semaphore_wait(barrier, len(partners))
    best = jnp.maximum(peak[:, :lane], peak[:, lane:])
    slot = 0
    stages = [[twin]] + [[near[axis, d] for d in (1, 3, 2)] for axis in (0, 1, 2)]
    for n, stage in enumerate(stages):
        peaks[slot] = best
        sends = []
        for k, target in enumerate(stage):
            copy = remote(peaks.at[slot], peaks.at[slot + 1 + k], peak_send.at[slot + k], peak_recv.at[slot + k], target)
            copy.start()
            sends.append(copy)
        for k, copy in enumerate(sends):
            copy.wait_recv()
            best = jnp.maximum(best, peaks[slot + 1 + k])
        for copy in sends:
            copy.wait_send()
        slot += 1 + len(stage)
    scale = jnp.max(best)
    ratio = code_levels / (scale + 1e-06)
    decode = (scale + 1e-06) / (code_levels * 128)

    def quantise(row, column):
        value = rot[pl.ds(pl.multiple_of(row, half), half), pl.ds(column, lane)]
        return jnp.floor(value * ratio + 0.5)

    def place(u, owner):
        order = lax.rem(u + owner, 3)
        first_row = owner * 1024 + lax.div(u, tiles) * half
        return order, first_row, pl.multiple_of(lax.rem(u, tiles) * lane, lane)

    def axes_of(order):
        a, b, c = order, lax.rem(order + 1, 3), lax.rem(order + 2, 3)
        return a, b, c, pick(a, x, y, z), pick(b, x, y, z), pick(c, x, y, z)

    def each_tile(order, first_row, work):
        a, b, c = order, lax.rem(order + 1, 3), lax.rem(order + 2, 3)
        in_b = [row_of(b, j) for j in range(4)]
        in_c = [row_of(c, k) for k in range(4)]

        def body(i, carry):
            start = first_row + row_of(a, i)
            for j in range(4):
                for k in range(4):
                    work(i, j, k, start + in_b[j] + in_c[k])
            return carry

        lax.fori_loop(0, 4, body, 0)

    def rs0(u):
        order, first_row, column = place(u, 1 - core)

        def work(i, j, k, row):
            other[u, i, j, k] = quantise(row, column).astype(jnp.bfloat16)

        each_tile(order, first_row, work)
        remote(other.at[u], core_in.at[u], rs_send.at[0], rs_core.at[u], twin).start()

    def rs1(u):
        order, first_row, column = place(u, core)
        drain(core_in.at[u], rs_core.at[u])

        def work(i, j, k, row):
            mine = quantise(row, column)
            s1[u, i, j, k] = (mine + core_in[u, i, j, k].astype(jnp.float32)).astype(jnp.bfloat16)

        each_tile(order, first_row, work)
        a, _, _, pa, _, _ = axes_of(order)
        up, down = along(a, 1), along(a, 3)
        far, pu, pd = step(pa, 2), step(pa, 1), step(pa, 3)
        lo, hi = pl.ds(0, 2), pl.ds(2, 2)
        remote(s1.at[u, far, lo], r1.at[u, 0], rs_send.at[1], rs_one.at[u], up).start()
        remote(s1.at[u, far, hi], r1.at[u, 1], rs_send.at[1], rs_one.at[u], down).start()
        remote(s1.at[u, pu, hi], r2.at[u, 0, hi], rs_send.at[1], rs_two.at[u], up).start()
        remote(s1.at[u, pd, lo], r2.at[u, 1, lo], rs_send.at[1], rs_two.at[u], down).start()

    def rs2(u):
        order, _, _ = place(u, core)
        a, _, _, pa, _, _ = axes_of(order)
        pu, pd = step(pa, 1), step(pa, 3)
        lo, hi = pl.ds(0, 2), pl.ds(2, 2)
        drain(r1.at[u], rs_one.at[u])
        f32 = jnp.float32
        s1[u, pu, lo] = (s1[u, pu, lo].astype(f32) + r1[u, 0].astype(f32)).astype(jnp.bfloat16)
        s1[u, pd, hi] = (s1[u, pd, hi].astype(f32) + r1[u, 1].astype(f32)).astype(jnp.bfloat16)
        remote(s1.at[u, pu, lo], r2.at[u, 0, lo], rs_send.at[2], rs_two.at[u], along(a, 1)).start()
        remote(s1.at[u, pd, hi], r2.at[u, 1, hi], rs_send.at[2], rs_two.at[u], along(a, 3)).start()

    def rs3(u):
        order, _, _ = place(u, core)
        _, b, _, pa, pb, _ = axes_of(order)
        drain(r2.at[u], rs_two.at[u])
        f32 = jnp.float32
        t1[u] = (s1[u, pa].astype(f32) + r2[u, 0].astype(f32) + r2[u, 1].astype(f32)).astype(jnp.bfloat16)
        for n, d in enumerate((1, 3, 2)):
            remote(t1.at[u, step(pb, d)], r3.at[u, n], rs_send.at[3], rs_three.at[u], along(b, d)).start()

    def rs4(u):
        order, _, _ = place(u, core)
        _, _, c, _, pb, pc = axes_of(order)
        drain(r3.at[u], rs_three.at[u])
        f32 = jnp.float32
        t2[u] = (
            t1[u, pb].astype(f32) + r3[u, 0].astype(f32) + r3[u, 1].astype(f32) + r3[u, 2].astype(f32)
        ).astype(jnp.bfloat16)
        for n, d in enumerate((1, 3, 2)):
            remote(t2.at[u, step(pc, d)], r4.at[u, n], rs_send.at[4], rs_four.at[u], along(c, d)).start()

    def rs5(u):
        order, _, column = place(u, core)
        pc = axes_of(order)[5]
        drain(r4.at[u], rs_four.at[u])
        f32 = jnp.float32
        value = t2[u, pc].astype(f32) + r4[u, 0].astype(f32) + r4[u, 1].astype(f32) + r4[u, 2].astype(f32)
        total[pl.ds(pl.multiple_of(lax.div(u, tiles) * half, half), half), pl.ds(column, lane)] = value

        @pl.when(lax.rem(u, tiles) == tiles - 1)
        def _():
            update(lax.div(u, tiles))

    owner = inner * 32 + outer

    def update(h):
        rows = pl.ds(pl.multiple_of(h * half, half), half)
        lows, highs = [], []
        for g in range(width // group):
            value = total[rows, g * group : (g + 1) * group]
            high = jnp.floor(value * (1.0 / 128.0) + 0.5)
            highs.append(high.astype(jnp.bfloat16))
            lows.append((value - high * 128.0).astype(jnp.bfloat16))
        stacked = jnp.concatenate(highs + lows, axis=0)
        product = jnp.dot(stacked, table[...], preferred_element_type=jnp.float32)
        parts = []
        for g in range(width // group):
            parts.append(
                product[g * half : (g + 1) * half] * 128.0 + product[(g + 4) * half : (g + 5) * half]
            )
        for g, turned in enumerate(butterfly(parts)):
            columns = slice(g * group, (g + 1) * group)
            offset = (owner * shard + h * half) * jnp.int32(wrap(width * hash_one)) + jnp.int32(wrap(g * group * hash_one))
            mean = turned * decode
            mean = jnp.where(negative(base[:half] + offset), -mean, mean)
            one = beta_one * adam_in[1, rows, columns] + (1.0 - beta_one) * mean
            two = beta_two * adam_in[2, rows, columns] + (1.0 - beta_two) * mean * mean
            old = adam_in[0, rows, columns]
            size = one / first_fix / (jnp.sqrt(two / second_fix) + adam_epsilon)
            new = old - learn_rate * (size + decay_rate * old)
            new_first[rows, columns] = one
            new_second[rows, columns] = two
            new_master[rows, columns] = new
            param = new.astype(jnp.bfloat16)
            for n in range(group // lane):
                u = h * tiles + g * (group // lane) + n
                order, _, _ = place(u, core)
                _, _, c, pa, pb, pc = axes_of(order)
                gath[u, pa, pb, pc] = param[:, n * lane : (n + 1) * lane]
                for d in (1, 3, 2):
                    remote(gath.at[u, pa, pb, pc], gath.at[u, pa, pb, pc], ag_send.at[0], ag_one.at[u], along(c, d)).start()

    def ag1(u):
        order, _, _ = place(u, core)
        _, b, _, pa, pb, _ = axes_of(order)
        drain(r4.at[u], ag_one.at[u])
        for d in (1, 3, 2):
            remote(gath.at[u, pa, pb], gath.at[u, pa, pb], ag_send.at[1], ag_two.at[u], along(b, d)).start()

    def ag2(u):
        order, _, _ = place(u, core)
        a, _, _, pa, _, _ = axes_of(order)
        drain(r3.at[u], ag_two.at[u])
        up, down = along(a, 1), along(a, 3)
        lo, hi = gath.at[u, pa, pl.ds(0, 2)], gath.at[u, pa, pl.ds(2, 2)]
        remote(lo, lo, ag_send.at[2], ag_near.at[u], up).start()
        remote(hi, hi, ag_send.at[2], ag_near.at[u], down).start()
        remote(hi, hi, ag_send.at[2], ag_far.at[u], up).start()
        remote(lo, lo, ag_send.at[2], ag_far.at[u], down).start()

    def ag3(u):
        order, _, _ = place(u, core)
        a, _, _, pa, _, _ = axes_of(order)
        drain(r1.at[u], ag_near.at[u])
        lo, hi = gath.at[u, step(pa, 3), pl.ds(0, 2)], gath.at[u, step(pa, 1), pl.ds(2, 2)]
        remote(lo, lo, ag_send.at[3], ag_far.at[u], along(a, 1)).start()
        remote(hi, hi, ag_send.at[3], ag_far.at[u], along(a, 3)).start()

    def lay_out(u, source, from_core):
        order, first_row, column = place(u, from_core)

        def work(i, j, k, row):
            out[pl.ds(pl.multiple_of(row, half), half), pl.ds(column, lane)] = source[u, i, j, k]

        each_tile(order, first_row, work)

    def ag4(u):
        drain(r2.at[u], ag_far.at[u])
        remote(gath.at[u], gath_other.at[u], ag_send.at[4], ag_core.at[u], twin).start()
        lay_out(u, gath, core)

    def ag5(u):
        drain(gath_other.at[u], ag_core.at[u])
        lay_out(u, gath_other, 1 - core)

    for copy in adam_copies:
        copy.wait()
    lead = tiles - 1 + RS[5]
    plan = [(ag5, lead + AG[5]), (ag4, lead + AG[4]), (ag3, lead + AG[3]), (ag2, lead + AG[2]), (ag1, lead + AG[1])]
    plan += [(rs5, RS[5]), (rs4, RS[4]), (rs3, RS[3]), (rs2, RS[2]), (rs1, RS[1]), (rs0, RS[0])]

    def tick(t, carry):
        for work, delay in plan:
            @pl.when(jnp.logical_and(t >= delay, t < delay + units))
            def _(work=work, delay=delay):
                work(t - delay)
        return carry

    lax.fori_loop(0, units + lead + AG[5], tick, 0)

    drain(other, rs_send.at[0])
    drain(r2, rs_send.at[1])
    drain(r1, rs_send.at[2])
    drain(r3, rs_send.at[3])
    drain(r4, rs_send.at[4])
    drain(r4, ag_send.at[0])
    drain(r3, ag_send.at[1])
    drain(r2, ag_send.at[2])
    drain(r1, ag_send.at[3])
    drain(gath, ag_send.at[4])


def per_device(gradients, master, first_moment, second_moment):
    bf16, f32 = jnp.bfloat16, jnp.float32
    anywhere = pl.BlockSpec(memory_space=pl.ANY)
    in_vmem = pl.BlockSpec(memory_space=pltpu.VMEM)
    piece = (4, half, lane)
    dma = pltpu.SemaphoreType.DMA
    params, new_master, new_first, new_second = pl.pallas_call(
        kernel,
        out_shape=(
            pltpu.VMEM((blocks, width), bf16),
            pltpu.VMEM((shard, width), f32),
            pltpu.VMEM((shard, width), f32),
            pltpu.VMEM((shard, width), f32),
        ),
        in_specs=[anywhere] * 4,
        out_specs=(in_vmem,) * 4,
        scratch_shapes=[
            pltpu.VMEM((blocks, width), f32),
            pltpu.VMEM((sub, group), jnp.int32),
            pltpu.VMEM((group, group), bf16),
            pltpu.VMEM((8, group), f32),
            pltpu.VMEM((14, 8, lane), f32),
            pltpu.VMEM((3, shard, width), f32),
            pltpu.VMEM((shard, width), f32),
            pltpu.VMEM((units, 4, 4) + piece, bf16),
            pltpu.VMEM((units, 4, 4) + piece, bf16),
            pltpu.VMEM((units, 4, 4) + piece, bf16),
            pltpu.VMEM((units, 2, 2) + piece, bf16),
            pltpu.VMEM((units, 2, 4) + piece, bf16),
            pltpu.VMEM((units, 4) + piece, bf16),
            pltpu.VMEM((units, 3) + piece, bf16),
            pltpu.VMEM((units,) + piece, bf16),
            pltpu.VMEM((units, 3, half, lane), bf16),
            pltpu.VMEM((units, 4, 4) + piece, bf16),
            pltpu.VMEM((units, 4, 4) + piece, bf16),
            dma((chunks,)), dma((3,)), dma((14,)), dma((14,)),
            dma((5,)), dma((units,)), dma((units,)), dma((units,)), dma((units,)), dma((units,)),
            dma((5,)), dma((units,)), dma((units,)), dma((units,)), dma((units,)), dma((units,)),
        ],
        compiler_params=pltpu.CompilerParams(
            collective_id=0, has_side_effects=True, vmem_limit_bytes=50 * 2**20
        ),
        cost_estimate=pl.CostEstimate(flops=2 * 2**32, bytes_accessed=2**25, transcendentals=0),
        name="reduce_step",
    )(gradients, master, first_moment, second_moment)
    return (new_master, new_first, new_second, params)


def solution(mesh):
    in_specs = (
        P(("inner", "outer"), None, None),
        P(("inner", "outer"), None),
        P(("inner", "outer"), None),
        P(("inner", "outer"), None),
    )
    out_specs = (
        P(("inner", "outer"), None),
        P(("inner", "outer"), None),
        P(("inner", "outer"), None),
        P(),
    )
    return jax.shard_map(
        per_device, mesh=mesh, in_specs=in_specs, out_specs=out_specs, check_vma=False
    )
```

```python
import functools
import math

import jax
import jax.numpy as jnp
from jax import lax
from jax.experimental import pallas as pl
from jax.experimental.pallas import tpu as pltpu
from jax.sharding import PartitionSpec as P

MESH = pl.DeviceIdType.MESH

code_levels = 127.0
beta_one = 0.9
beta_two = 0.95
learn_rate = 0.002
decay_rate = 0.1
adam_epsilon = 1e-08
first_fix = 1.0 - 0.9**10
second_fix = 1.0 - 0.95**10

blocks = 4096
width = 1024
group = 256
shard = 32
half = 16
lane = 128
tiles = width // lane
units = 2 * tiles
chunk = 512
chunks = blocks // chunk
sub = 512

hash_one = -1640531535
hash_two = ((-2048144777 << 18) & 0xFFFFFFFF) - (1 << 32 if ((-2048144777 << 18) & 0x80000000) else 0)


def wrap(value):
    value &= 0xFFFFFFFF
    return value - (1 << 32) if value & 0x80000000 else value


RS = (0, 8, 13, 17, 23, 29)
AG = (0, 3, 9, 13, 18, 21)


def negative(hashed):
    mixed = jnp.bitwise_xor(hashed, jnp.right_shift(hashed, 15))
    return mixed * jnp.int32(hash_two) < 0


def butterfly(parts):
    p0, p1, p2, p3 = parts
    a, b, c, d = p0 + p1, p0 - p1, p2 + p3, p2 - p3
    return a + c, b + d, a - c, b - d


def pick(order, v0, v1, v2):
    return jnp.where(order == 0, v0, jnp.where(order == 1, v1, v2))


def row_of(axis, v):
    if isinstance(v, int):
        return pick(axis, v * shard, (v % 2) * 128 + (v // 2) * 2048, v * 256)
    return pick(axis, v * shard, lax.rem(v, 2) * 128 + lax.div(v, 2) * 2048, v * 256)


def kernel(
    grad, master, first, second,
    out, fresh,
    rot, base, table, peak, peaks_one, peaks_two, adam_in, total,
    other, core_in, s1, r1, r2, t1, r3, t2, r4, gath, gath_other,
    grad_sem, adam_sem, peak_send, peak_recv,
    rs_send, rs_core, rs_one, rs_two, rs_three, rs_four,
    ag_send, ag_one, ag_two, ag_near, ag_far, ag_core,
):
    inner, outer = lax.axis_index("inner"), lax.axis_index("outer")
    core = lax.rem(inner, 2)
    x = lax.rem(outer, 4)
    y = lax.div(inner, 2) * 2 + lax.rem(lax.div(outer, 4), 2)
    z = lax.div(outer, 8)

    def device(xx, yy, zz, cc):
        return (lax.div(yy, 2) * 2 + cc, zz * 8 + lax.rem(yy, 2) * 4 + xx)

    def step(v, d):
        return lax.rem(v + d, 4)

    near = {}
    for d in (1, 2, 3):
        near[0, d] = device(step(x, d), y, z, core)
        near[1, d] = device(x, step(y, d), z, core)
        near[2, d] = device(x, y, step(z, d), core)
    twin = device(x, y, z, 1 - core)

    def along(axis, d):
        return tuple(pick(axis, near[0, d][n], near[1, d][n], near[2, d][n]) for n in (0, 1))

    def remote(src, dst, send, recv, target):
        return pltpu.make_async_remote_copy(
            src_ref=src, dst_ref=dst, send_sem=send, recv_sem=recv, device_id=target, device_id_type=MESH
        )

    def drain(ref, sem):
        pltpu.make_async_copy(ref, ref, sem).wait()

    barrier = pltpu.get_barrier_semaphore()
    column = [device(x, y, step(z, d), c) for d in range(4) for c in (core, 1 - core)][1:]
    plane = [device(step(x, d), step(y, e), z, core) for d in range(4) for e in range(4)][1:]
    partners = column + plane
    for partner in partners:
        pl.semaphore_signal(barrier, inc=1, device_id=partner, device_id_type=MESH)

    def grad_copy(i):
        rows = pl.ds(pl.multiple_of(i * chunk, chunk), chunk)
        return pltpu.make_async_copy(grad.at[0, rows], out.at[rows], grad_sem.at[i])

    def start_grad(i, carry):
        grad_copy(i).start()
        return carry

    lax.fori_loop(0, chunks, start_grad, 0)
    adam_copies = [
        pltpu.make_async_copy(ref, adam_in.at[n], adam_sem.at[n]) for n, ref in enumerate((master, first, second))
    ]
    for copy in adam_copies:
        copy.start()

    rows_i = lax.broadcasted_iota(jnp.int32, (group, group), 0)
    cols_i = lax.broadcasted_iota(jnp.int32, (group, group), 1)
    common = jnp.bitwise_and(rows_i, cols_i)
    for shift in (4, 2, 1):
        common = jnp.bitwise_xor(common, jnp.right_shift(common, shift))
    parity = jnp.bitwise_and(common, 1)
    table[...] = ((1 - 2 * parity).astype(jnp.float32) / math.sqrt(width)).astype(jnp.bfloat16)
    base[...] = (
        lax.broadcasted_iota(jnp.int32, (sub, group), 0) * jnp.int32(wrap(width * hash_one))
        + lax.broadcasted_iota(jnp.int32, (sub, group), 1) * jnp.int32(hash_one)
    )
    peak[...] = jnp.zeros_like(peak)

    def rotate(i, carry):
        grad_copy(i).wait()
        rows = pl.ds(pl.multiple_of(i * sub, sub), sub)
        pieces = []
        for g in range(width // group):
            offset = i * jnp.int32(wrap(sub * width * hash_one)) + jnp.int32(wrap(g * group * hash_one))
            sign = jnp.where(negative(base[...] + offset), -1.0, 1.0).astype(jnp.bfloat16)
            flipped = out[rows, g * group : (g + 1) * group] * sign
            pieces.append(flipped)
        turned = jnp.dot(jnp.concatenate(pieces, axis=0), table[...], preferred_element_type=jnp.float32)
        pieces = [turned[g * sub : (g + 1) * sub] for g in range(width // group)]
        top = peak[...]
        for g, piece in enumerate(butterfly(pieces)):
            rot[rows, g * group : (g + 1) * group] = piece
            top = jnp.maximum(top, jnp.max(jnp.abs(piece).reshape(sub // 8, 8, group), axis=0))
        peak[...] = top
        return carry

    lax.fori_loop(0, blocks // sub, rotate, 0)

    pl.semaphore_wait(barrier, len(partners))
    best = jnp.max(jnp.maximum(peak[:, :lane], peak[:, lane:]), axis=0, keepdims=True)
    for n, (stage, box) in enumerate(((column, peaks_one), (plane, peaks_two))):
        box[0, :1] = best
        for k, target in enumerate(stage):
            remote(box.at[0, :1], box.at[1 + k, :1], peak_send.at[n], peak_recv.at[n], target).start()
        arrived = box.at[pl.ds(1, len(stage)), :1]
        drain(arrived, peak_recv.at[n])
        for k in range(len(stage)):
            best = jnp.maximum(best, box[1 + k, :1])
    scale = jnp.max(best)
    ratio = code_levels / (scale + 1e-06)
    decode = (scale + 1e-06) / (code_levels * 128)

    def quantise(row, column):
        value = rot[pl.ds(pl.multiple_of(row, half), half), pl.ds(column, lane)]
        return jnp.floor(value * ratio + 0.5)

    def place(u, owner):
        order = lax.rem(u + owner, 3)
        first_row = owner * 1024 + lax.div(u, tiles) * half
        return order, first_row, pl.multiple_of(lax.rem(u, tiles) * lane, lane)

    def axes_of(order):
        a, b, c = order, lax.rem(order + 1, 3), lax.rem(order + 2, 3)
        return a, b, c, pick(a, x, y, z), pick(b, x, y, z), pick(c, x, y, z)

    def each_tile(order, first_row, work):
        a, b, c = order, lax.rem(order + 1, 3), lax.rem(order + 2, 3)
        in_b = [row_of(b, j) for j in range(4)]
        in_c = [row_of(c, k) for k in range(4)]

        def body(i, carry):
            start = first_row + row_of(a, i)
            for j in range(4):
                for k in range(4):
                    work(i, j, k, start + in_b[j] + in_c[k])
            return carry

        lax.fori_loop(0, 4, body, 0)

    def rs0(u):
        order, first_row, column = place(u, 1 - core)

        def work(i, j, k, row):
            other[u, i, j, k] = quantise(row, column).astype(jnp.bfloat16)

        each_tile(order, first_row, work)
        remote(other.at[u], core_in.at[u], rs_send.at[0], rs_core.at[u], twin).start()

    def rs1(u):
        order, first_row, column = place(u, core)
        drain(core_in.at[u], rs_core.at[u])

        def work(i, j, k, row):
            mine = quantise(row, column)
            s1[u, i, j, k] = (mine + core_in[u, i, j, k].astype(jnp.float32)).astype(jnp.bfloat16)

        each_tile(order, first_row, work)
        a, _, _, pa, _, _ = axes_of(order)
        up, down = along(a, 1), along(a, 3)
        far, pu, pd = step(pa, 2), step(pa, 1), step(pa, 3)
        lo, hi = pl.ds(0, 2), pl.ds(2, 2)
        remote(s1.at[u, far, lo], r1.at[u, 0], rs_send.at[1], rs_one.at[u], up).start()
        remote(s1.at[u, far, hi], r1.at[u, 1], rs_send.at[1], rs_one.at[u], down).start()
        remote(s1.at[u, pu, hi], r2.at[u, 0, hi], rs_send.at[1], rs_two.at[u], up).start()
        remote(s1.at[u, pd, lo], r2.at[u, 1, lo], rs_send.at[1], rs_two.at[u], down).start()

    def rs2(u):
        order, _, _ = place(u, core)
        a, _, _, pa, _, _ = axes_of(order)
        pu, pd = step(pa, 1), step(pa, 3)
        lo, hi = pl.ds(0, 2), pl.ds(2, 2)
        drain(r1.at[u], rs_one.at[u])
        f32 = jnp.float32
        s1[u, pu, lo] = (s1[u, pu, lo].astype(f32) + r1[u, 0].astype(f32)).astype(jnp.bfloat16)
        s1[u, pd, hi] = (s1[u, pd, hi].astype(f32) + r1[u, 1].astype(f32)).astype(jnp.bfloat16)
        remote(s1.at[u, pu, lo], r2.at[u, 0, lo], rs_send.at[2], rs_two.at[u], along(a, 1)).start()
        remote(s1.at[u, pd, hi], r2.at[u, 1, hi], rs_send.at[2], rs_two.at[u], along(a, 3)).start()

    def rs3(u):
        order, _, _ = place(u, core)
        _, b, _, pa, pb, _ = axes_of(order)
        drain(r2.at[u], rs_two.at[u])
        f32 = jnp.float32
        t1[u] = (s1[u, pa].astype(f32) + r2[u, 0].astype(f32) + r2[u, 1].astype(f32)).astype(jnp.bfloat16)
        for n, d in enumerate((1, 3, 2)):
            remote(t1.at[u, step(pb, d)], r3.at[u, n], rs_send.at[3], rs_three.at[u], along(b, d)).start()

    def rs4(u):
        order, _, _ = place(u, core)
        _, _, c, _, pb, pc = axes_of(order)
        drain(r3.at[u], rs_three.at[u])
        f32 = jnp.float32
        t2[u] = (
            t1[u, pb].astype(f32) + r3[u, 0].astype(f32) + r3[u, 1].astype(f32) + r3[u, 2].astype(f32)
        ).astype(jnp.bfloat16)
        for n, d in enumerate((1, 3, 2)):
            remote(t2.at[u, step(pc, d)], r4.at[u, n], rs_send.at[4], rs_four.at[u], along(c, d)).start()

    def rs5(u):
        order, _, column = place(u, core)
        pc = axes_of(order)[5]
        drain(r4.at[u], rs_four.at[u])
        f32 = jnp.float32
        value = t2[u, pc].astype(f32) + r4[u, 0].astype(f32) + r4[u, 1].astype(f32) + r4[u, 2].astype(f32)
        total[pl.ds(pl.multiple_of(lax.div(u, tiles) * half, half), half), pl.ds(column, lane)] = value

        @pl.when(lax.rem(u, tiles) == tiles - 1)
        def _():
            update(lax.div(u, tiles))

    owner = inner * 32 + outer

    def update(h):
        rows = pl.ds(pl.multiple_of(h * half, half), half)
        lows, highs = [], []
        for g in range(width // group):
            value = total[rows, g * group : (g + 1) * group]
            high = jnp.floor(value * (1.0 / 128.0) + 0.5)
            highs.append(high.astype(jnp.bfloat16))
            lows.append((value - high * 128.0).astype(jnp.bfloat16))
        stacked = jnp.concatenate(highs + lows, axis=0)
        product = jnp.dot(stacked, table[...], preferred_element_type=jnp.float32)
        parts = []
        for g in range(width // group):
            parts.append(
                product[g * half : (g + 1) * half] * 128.0 + product[(g + 4) * half : (g + 5) * half]
            )
        for g, turned in enumerate(butterfly(parts)):
            columns = slice(g * group, (g + 1) * group)
            offset = (owner * shard + h * half) * jnp.int32(wrap(width * hash_one)) + jnp.int32(wrap(g * group * hash_one))
            mean = turned * decode
            mean = jnp.where(negative(base[:half] + offset), -mean, mean)
            one = beta_one * adam_in[1, rows, columns] + (1.0 - beta_one) * mean
            two = beta_two * adam_in[2, rows, columns] + (1.0 - beta_two) * mean * mean
            old = adam_in[0, rows, columns]
            size = one / first_fix / (jnp.sqrt(two / second_fix) + adam_epsilon)
            new = old - learn_rate * (size + decay_rate * old)
            fresh[1, rows, columns] = one
            fresh[2, rows, columns] = two
            fresh[0, rows, columns] = new
            param = new.astype(jnp.bfloat16)
            for n in range(group // lane):
                u = h * tiles + g * (group // lane) + n
                order, _, _ = place(u, core)
                _, _, c, pa, pb, pc = axes_of(order)
                gath[u, pa, pb, pc] = param[:, n * lane : (n + 1) * lane]
                for d in (1, 3, 2):
                    remote(gath.at[u, pa, pb, pc], gath.at[u, pa, pb, pc], ag_send.at[0], ag_one.at[u], along(c, d)).start()

    def ag1(u):
        order, _, _ = place(u, core)
        _, b, _, pa, pb, _ = axes_of(order)
        drain(r4.at[u], ag_one.at[u])
        for d in (1, 3, 2):
            remote(gath.at[u, pa, pb], gath.at[u, pa, pb], ag_send.at[1], ag_two.at[u], along(b, d)).start()

    def ag2(u):
        order, _, _ = place(u, core)
        a, _, _, pa, _, _ = axes_of(order)
        drain(r3.at[u], ag_two.at[u])
        up, down = along(a, 1), along(a, 3)
        lo, hi = gath.at[u, pa, pl.ds(0, 2)], gath.at[u, pa, pl.ds(2, 2)]
        remote(lo, lo, ag_send.at[2], ag_near.at[u], up).start()
        remote(hi, hi, ag_send.at[2], ag_near.at[u], down).start()
        remote(hi, hi, ag_send.at[2], ag_far.at[u], up).start()
        remote(lo, lo, ag_send.at[2], ag_far.at[u], down).start()

    def ag3(u):
        order, _, _ = place(u, core)
        a, _, _, pa, _, _ = axes_of(order)
        drain(r1.at[u], ag_near.at[u])
        lo, hi = gath.at[u, step(pa, 3), pl.ds(0, 2)], gath.at[u, step(pa, 1), pl.ds(2, 2)]
        remote(lo, lo, ag_send.at[3], ag_far.at[u], along(a, 1)).start()
        remote(hi, hi, ag_send.at[3], ag_far.at[u], along(a, 3)).start()

    def lay_out(u, source, from_core):
        order, first_row, column = place(u, from_core)

        def work(i, j, k, row):
            out[pl.ds(pl.multiple_of(row, half), half), pl.ds(column, lane)] = source[u, i, j, k]

        each_tile(order, first_row, work)

    def ag4(u):
        drain(r2.at[u], ag_far.at[u])
        remote(gath.at[u], gath_other.at[u], ag_send.at[4], ag_core.at[u], twin).start()
        lay_out(u, gath, core)

    def ag5(u):
        drain(gath_other.at[u], ag_core.at[u])
        lay_out(u, gath_other, 1 - core)

    for copy in adam_copies:
        copy.wait()
    lead = tiles - 1 + RS[5]
    plan = [(ag5, lead + AG[5]), (ag4, lead + AG[4]), (ag3, lead + AG[3]), (ag2, lead + AG[2]), (ag1, lead + AG[1])]
    plan += [(rs5, RS[5]), (rs4, RS[4]), (rs3, RS[3]), (rs2, RS[2]), (rs1, RS[1]), (rs0, RS[0])]

    plan = plan[::-1]

    def tick(t, carry):
        for work, delay in plan:
            @pl.when(jnp.logical_and(t >= delay, t < delay + units))
            def _(work=work, delay=delay):
                work(t - delay)
        return carry

    lax.fori_loop(0, units + lead + AG[5], tick, 0)

    for n, box in enumerate((peaks_one, peaks_two)):
        drain(box.at[pl.ds(1, (7, 15)[n]), :1], peak_send.at[n])
    drain(other, rs_send.at[0])
    drain(r2, rs_send.at[1])
    drain(r1, rs_send.at[2])
    drain(r3, rs_send.at[3])
    drain(r4, rs_send.at[4])
    drain(r4, ag_send.at[0])
    drain(r3, ag_send.at[1])
    drain(r2, ag_send.at[2])
    drain(r1, ag_send.at[3])
    drain(gath, ag_send.at[4])


def per_device(gradients, master, first_moment, second_moment):
    bf16, f32 = jnp.bfloat16, jnp.float32
    anywhere = pl.BlockSpec(memory_space=pl.ANY)
    in_vmem = pl.BlockSpec(memory_space=pltpu.VMEM)
    piece = (4, half, lane)
    dma = pltpu.SemaphoreType.DMA
    params, fresh = pl.pallas_call(
        kernel,
        out_shape=(
            pltpu.VMEM((blocks, width), bf16),
            pltpu.VMEM((3, shard, width), f32),
        ),
        in_specs=[anywhere] * 4,
        out_specs=(in_vmem,) * 2,
        scratch_shapes=[
            pltpu.VMEM((blocks, width), f32),
            pltpu.VMEM((sub, group), jnp.int32),
            pltpu.VMEM((group, group), bf16),
            pltpu.VMEM((8, group), f32),
            pltpu.VMEM((8, 8, lane), f32),
            pltpu.VMEM((16, 8, lane), f32),
            pltpu.VMEM((3, shard, width), f32),
            pltpu.VMEM((shard, width), f32),
            pltpu.VMEM((units, 4, 4) + piece, bf16),
            pltpu.VMEM((units, 4, 4) + piece, bf16),
            pltpu.VMEM((units, 4, 4) + piece, bf16),
            pltpu.VMEM((units, 2, 2) + piece, bf16),
            pltpu.VMEM((units, 2, 4) + piece, bf16),
            pltpu.VMEM((units, 4) + piece, bf16),
            pltpu.VMEM((units, 3) + piece, bf16),
            pltpu.VMEM((units,) + piece, bf16),
            pltpu.VMEM((units, 3, half, lane), bf16),
            pltpu.VMEM((units, 4, 4) + piece, bf16),
            pltpu.VMEM((units, 4, 4) + piece, bf16),
            dma((chunks,)), dma((3,)), dma((2,)), dma((2,)),
            dma((5,)), dma((units,)), dma((units,)), dma((units,)), dma((units,)), dma((units,)),
            dma((5,)), dma((units,)), dma((units,)), dma((units,)), dma((units,)), dma((units,)),
        ],
        compiler_params=pltpu.CompilerParams(
            collective_id=0, has_side_effects=True, vmem_limit_bytes=50 * 2**20
        ),
        cost_estimate=pl.CostEstimate(flops=2 * 2**32, bytes_accessed=2**25, transcendentals=0),
        name="reduce_step",
    )(gradients, master, first_moment, second_moment)
    return (fresh[0], fresh[1], fresh[2], params)


def solution(mesh):
    in_specs = (
        P(("inner", "outer"), None, None),
        P(("inner", "outer"), None),
        P(("inner", "outer"), None),
        P(("inner", "outer"), None),
    )
    out_specs = (
        P(("inner", "outer"), None),
        P(("inner", "outer"), None),
        P(("inner", "outer"), None),
        P(),
    )
    return jax.shard_map(
        per_device, mesh=mesh, in_specs=in_specs, out_specs=out_specs, check_vma=False
    )
```

```python
import functools
import math

import jax
import jax.numpy as jnp
import numpy as np
from jax import lax
from jax.experimental import pallas as pl
from jax.experimental.pallas import tpu as pltpu
from jax.sharding import PartitionSpec as P

MESH = pl.DeviceIdType.MESH

code_levels = 127.0
beta_one = 0.9
beta_two = 0.95
learn_rate = 0.002
decay_rate = 0.1
adam_epsilon = 1e-08
first_fix = 1.0 - 0.9**10
second_fix = 1.0 - 0.95**10

blocks = 4096
width = 1024
group = 256
shard = 32
half = 16
lane = 128
rows_of = 8
wide = 2 * lane
tiles = width // wide
units = shard // rows_of * tiles
chunk = 512
chunks = blocks // chunk
sub = 512

hash_one = -1640531535
hash_two = ((-2048144777 << 18) & 0xFFFFFFFF) - (1 << 32 if ((-2048144777 << 18) & 0x80000000) else 0)


def wrap(value):
    value &= 0xFFFFFFFF
    return value - (1 << 32) if value & 0x80000000 else value


RS = (0, 9, 14, 18, 24, 30)
AG = (0, 4, 10, 15, 20, 23)


def sign_words():
    at = np.arange(blocks * width, dtype=np.uint32).reshape(blocks, width)
    hashed = (at * np.uint32(hash_one & 0xFFFFFFFF)).view(np.int32)
    hashed = np.bitwise_xor(hashed, np.right_shift(hashed, 15)).view(np.uint32) * np.uint32(-2048144777 & 0xFFFFFFFF)
    bits = ((hashed >> np.uint32(13)) & np.uint32(1)).reshape(blocks // 256, 32, 8, width)
    return (bits << np.arange(32, dtype=np.uint32)[None, :, None, None]).sum(axis=1, dtype=np.uint32).view(np.int32)


def negative(hashed):
    mixed = jnp.bitwise_xor(hashed, jnp.right_shift(hashed, 15))
    return mixed * jnp.int32(hash_two) < 0


def butterfly(parts):
    p0, p1, p2, p3 = parts
    a, b, c, d = p0 + p1, p0 - p1, p2 + p3, p2 - p3
    return a + c, b + d, a - c, b - d


def pick(order, v0, v1, v2):
    return jnp.where(order == 0, v0, jnp.where(order == 1, v1, v2))


def row_of(axis, v):
    if isinstance(v, int):
        return pick(axis, v * shard, (v % 2) * 128 + (v // 2) * 2048, v * 256)
    return pick(axis, v * shard, lax.rem(v, 2) * 128 + lax.div(v, 2) * 2048, v * 256)


def kernel(
    grad, master, first, second, words,
    out, fresh,
    rot, base, signs, table, peak, peaks_one, peaks_two, adam_in, total,
    other, core_in, s1, r1, r2, t1, r3, t2, r4, gath, gath_other,
    grad_sem, sign_sem, adam_sem, peak_send, peak_recv,
    rs_send, rs_core, rs_one, rs_two, rs_three, rs_four,
    ag_send, ag_one, ag_two, ag_near, ag_far, ag_core,
):
    inner, outer = lax.axis_index("inner"), lax.axis_index("outer")
    core = lax.rem(inner, 2)
    x = lax.rem(outer, 4)
    y = lax.div(inner, 2) * 2 + lax.rem(lax.div(outer, 4), 2)
    z = lax.div(outer, 8)

    def device(xx, yy, zz, cc):
        return (lax.div(yy, 2) * 2 + cc, zz * 8 + lax.rem(yy, 2) * 4 + xx)

    def step(v, d):
        return lax.rem(v + d, 4)

    near = {}
    for d in (1, 2, 3):
        near[0, d] = device(step(x, d), y, z, core)
        near[1, d] = device(x, step(y, d), z, core)
        near[2, d] = device(x, y, step(z, d), core)
    twin = device(x, y, z, 1 - core)

    def along(axis, d):
        return tuple(pick(axis, near[0, d][n], near[1, d][n], near[2, d][n]) for n in (0, 1))

    def remote(src, dst, send, recv, target):
        return pltpu.make_async_remote_copy(
            src_ref=src, dst_ref=dst, send_sem=send, recv_sem=recv, device_id=target, device_id_type=MESH
        )

    def drain(ref, sem):
        pltpu.make_async_copy(ref, ref, sem).wait()

    barrier = pltpu.get_barrier_semaphore()
    column = [device(x, y, step(z, d), c) for d in range(4) for c in (core, 1 - core)][1:]
    plane = [device(step(x, d), step(y, e), z, core) for d in range(4) for e in range(4)][1:]
    partners = column + plane
    for partner in partners:
        pl.semaphore_signal(barrier, inc=1, device_id=partner, device_id_type=MESH)

    def grad_copy(i):
        rows = pl.ds(pl.multiple_of(i * chunk, chunk), chunk)
        return pltpu.make_async_copy(grad.at[0, rows], out.at[rows], grad_sem.at[i])

    def start_grad(i, carry):
        grad_copy(i).start()
        return carry

    sign_copy = pltpu.make_async_copy(words, signs, sign_sem.at[0])
    sign_copy.start()
    lax.fori_loop(0, chunks, start_grad, 0)
    adam_copies = [
        pltpu.make_async_copy(ref, adam_in.at[n], adam_sem.at[n]) for n, ref in enumerate((master, first, second))
    ]
    for copy in adam_copies:
        copy.start()

    rows_i = lax.broadcasted_iota(jnp.int32, (group, group), 0)
    cols_i = lax.broadcasted_iota(jnp.int32, (group, group), 1)
    common = jnp.bitwise_and(rows_i, cols_i)
    for shift in (4, 2, 1):
        common = jnp.bitwise_xor(common, jnp.right_shift(common, shift))
    parity = jnp.bitwise_and(common, 1)
    table[...] = ((1 - 2 * parity).astype(jnp.float32) / math.sqrt(width)).astype(jnp.bfloat16)
    base[...] = (
        lax.broadcasted_iota(jnp.int32, (rows_of, group), 0) * jnp.int32(wrap(width * hash_one))
        + lax.broadcasted_iota(jnp.int32, (rows_of, group), 1) * jnp.int32(hash_one)
    )
    peak[...] = jnp.zeros_like(peak)

    sign_copy.wait()

    def rotate(i, carry):
        grad_copy(i).wait()
        rows = pl.ds(pl.multiple_of(i * sub, sub), sub)
        pieces = []
        for g in range(width // group):
            held = [signs[i * (sub // 256) + n, :, g * group : (g + 1) * group] for n in range(sub // 256)]
            shifted = [jnp.left_shift(word, 31 - r) for word in held for r in range(32)]
            sign = jnp.where(jnp.concatenate(shifted, axis=0) < 0, -1.0, 1.0).astype(jnp.bfloat16)
            flipped = out[rows, g * group : (g + 1) * group] * sign
            pieces.append(flipped)
        turned = jnp.dot(jnp.concatenate(pieces, axis=0), table[...], preferred_element_type=jnp.float32)
        pieces = [turned[g * sub : (g + 1) * sub] for g in range(width // group)]
        top = peak[...]
        for g, piece in enumerate(butterfly(pieces)):
            rot[rows, g * group : (g + 1) * group] = piece
            top = jnp.maximum(top, jnp.max(jnp.abs(piece).reshape(sub // 8, 8, group), axis=0))
        peak[...] = top
        return carry

    lax.fori_loop(0, blocks // sub, rotate, 0)

    pl.semaphore_wait(barrier, len(partners))
    best = jnp.max(jnp.maximum(peak[:, :lane], peak[:, lane:]), axis=0, keepdims=True)
    for n, (stage, box) in enumerate(((column, peaks_one), (plane, peaks_two))):
        box[0, :1] = best
        for k, target in enumerate(stage):
            remote(box.at[0, :1], box.at[1 + k, :1], peak_send.at[n], peak_recv.at[n], target).start()
        arrived = box.at[pl.ds(1, len(stage)), :1]
        drain(arrived, peak_recv.at[n])
        for k in range(len(stage)):
            best = jnp.maximum(best, box[1 + k, :1])
    scale = jnp.max(best)
    ratio = code_levels / (scale + 1e-06)
    decode = (scale + 1e-06) / (code_levels * 128)

    def fold(value):
        return jnp.concatenate([value[:, :lane], value[:, lane:]], axis=0)

    def quantise(row, column):
        value = rot[pl.ds(pl.multiple_of(row, rows_of), rows_of), pl.ds(column, wide)]
        return fold(jnp.floor(value * ratio + 0.5))

    def place(u, owner):
        order = lax.rem(u + owner, 3)
        first_row = owner * 1024 + lax.div(u, tiles) * rows_of
        return order, first_row, pl.multiple_of(lax.rem(u, tiles) * wide, wide)

    def axes_of(order):
        a, b, c = order, lax.rem(order + 1, 3), lax.rem(order + 2, 3)
        return a, b, c, pick(a, x, y, z), pick(b, x, y, z), pick(c, x, y, z)

    def each_tile(order, first_row, work):
        a, b, c = order, lax.rem(order + 1, 3), lax.rem(order + 2, 3)
        in_b = [row_of(b, j) for j in range(4)]
        in_c = [row_of(c, k) for k in range(4)]

        def body(i, carry):
            start = first_row + row_of(a, i)
            for j in range(4):
                for k in range(4):
                    work(i, j, k, start + in_b[j] + in_c[k])
            return carry

        lax.fori_loop(0, 4, body, 0)

    def rs0(u):
        order, first_row, column = place(u, 1 - core)

        def work(i, j, k, row):
            other[u, i, j, k] = quantise(row, column).astype(jnp.bfloat16)

        each_tile(order, first_row, work)
        remote(other.at[u], core_in.at[u], rs_send.at[0], rs_core.at[u], twin).start()

    def rs1(u):
        order, first_row, column = place(u, core)
        drain(core_in.at[u], rs_core.at[u])

        def work(i, j, k, row):
            mine = quantise(row, column)
            s1[u, i, j, k] = (mine + core_in[u, i, j, k].astype(jnp.float32)).astype(jnp.bfloat16)

        each_tile(order, first_row, work)
        a, _, _, pa, _, _ = axes_of(order)
        up, down = along(a, 1), along(a, 3)
        far, pu, pd = step(pa, 2), step(pa, 1), step(pa, 3)
        lo, hi = pl.ds(0, 2), pl.ds(2, 2)
        remote(s1.at[u, far, lo], r1.at[u, 0], rs_send.at[1], rs_one.at[u], up).start()
        remote(s1.at[u, far, hi], r1.at[u, 1], rs_send.at[1], rs_one.at[u], down).start()
        remote(s1.at[u, pu, hi], r2.at[u, 0, hi], rs_send.at[1], rs_two.at[u], up).start()
        remote(s1.at[u, pd, lo], r2.at[u, 1, lo], rs_send.at[1], rs_two.at[u], down).start()

    def rs2(u):
        order, _, _ = place(u, core)
        a, _, _, pa, _, _ = axes_of(order)
        pu, pd = step(pa, 1), step(pa, 3)
        lo, hi = pl.ds(0, 2), pl.ds(2, 2)
        drain(r1.at[u], rs_one.at[u])
        s1[u, pu, lo] += r1[u, 0]
        s1[u, pd, hi] += r1[u, 1]
        remote(s1.at[u, pu, lo], r2.at[u, 0, lo], rs_send.at[2], rs_two.at[u], along(a, 1)).start()
        remote(s1.at[u, pd, hi], r2.at[u, 1, hi], rs_send.at[2], rs_two.at[u], along(a, 3)).start()

    def rs3(u):
        order, _, _ = place(u, core)
        _, b, _, pa, pb, _ = axes_of(order)
        drain(r2.at[u], rs_two.at[u])
        f32 = jnp.float32
        t1[u] = (s1[u, pa].astype(f32) + r2[u, 0].astype(f32) + r2[u, 1].astype(f32)).astype(jnp.bfloat16)
        for n, d in enumerate((1, 3, 2)):
            remote(t1.at[u, step(pb, d)], r3.at[u, n], rs_send.at[3], rs_three.at[u], along(b, d)).start()

    def rs4(u):
        order, _, _ = place(u, core)
        _, _, c, _, pb, pc = axes_of(order)
        drain(r3.at[u], rs_three.at[u])
        f32 = jnp.float32
        t2[u] = (
            t1[u, pb].astype(f32) + r3[u, 0].astype(f32) + r3[u, 1].astype(f32) + r3[u, 2].astype(f32)
        ).astype(jnp.bfloat16)
        for n, d in enumerate((1, 3, 2)):
            remote(t2.at[u, step(pc, d)], r4.at[u, n], rs_send.at[4], rs_four.at[u], along(c, d)).start()

    def rs5(u):
        order, _, column = place(u, core)
        pc = axes_of(order)[5]
        drain(r4.at[u], rs_four.at[u])
        f32 = jnp.float32
        value = t2[u, pc].astype(f32) + r4[u, 0].astype(f32) + r4[u, 1].astype(f32) + r4[u, 2].astype(f32)
        rows = pl.ds(pl.multiple_of(lax.div(u, tiles) * rows_of, rows_of), rows_of)
        total[rows, pl.ds(column, lane)] = value[:rows_of]
        total[rows, pl.ds(column + lane, lane)] = value[rows_of:]

        @pl.when(lax.rem(u, tiles) == tiles - 1)
        def _():
            update(lax.div(u, tiles))

    owner = inner * 32 + outer

    def update(h):
        rows = pl.ds(pl.multiple_of(h * rows_of, rows_of), rows_of)
        value = jnp.concatenate([total[rows, g * group : (g + 1) * group] for g in range(width // group)], axis=0)
        high = jnp.floor(value * (1.0 / 128.0) + 0.5)
        stacked = jnp.concatenate([high, value - high * 128.0], axis=0).astype(jnp.bfloat16)
        product = jnp.dot(stacked, table[...], preferred_element_type=jnp.float32)
        product = product[: 4 * rows_of] * 128.0 + product[4 * rows_of :]
        parts = [product[g * rows_of : (g + 1) * rows_of] for g in range(width // group)]
        for g, turned in enumerate(butterfly(parts)):
            columns = slice(g * group, (g + 1) * group)
            offset = (owner * shard + h * rows_of) * jnp.int32(wrap(width * hash_one)) + jnp.int32(wrap(g * group * hash_one))
            mean = turned * decode
            mean = jnp.where(negative(base[...] + offset), -mean, mean)
            one = beta_one * adam_in[1, rows, columns] + (1.0 - beta_one) * mean
            two = beta_two * adam_in[2, rows, columns] + (1.0 - beta_two) * mean * mean
            old = adam_in[0, rows, columns]
            size = one / first_fix / (jnp.sqrt(two / second_fix) + adam_epsilon)
            new = old - learn_rate * (size + decay_rate * old)
            fresh[1, rows, columns] = one
            fresh[2, rows, columns] = two
            fresh[0, rows, columns] = new
            u = h * tiles + g
            order, _, _ = place(u, core)
            _, _, c, pa, pb, pc = axes_of(order)
            mine = pa * 16 + pb * 4 + pc
            gath[u, mine] = fold(new).astype(jnp.bfloat16)
            for d in (1, 3, 2):
                remote(gath.at[u, mine], gath.at[u, mine], ag_send.at[0], ag_one.at[u], along(c, d)).start()

    def ag1(u):
        order, _, _ = place(u, core)
        _, b, _, pa, pb, _ = axes_of(order)
        drain(r4.at[u], ag_one.at[u])
        row = gath.at[u, pl.ds(pa * 16 + pb * 4, 4)]
        for d in (1, 3, 2):
            remote(row, row, ag_send.at[1], ag_two.at[u], along(b, d)).start()

    def ag2(u):
        order, _, _ = place(u, core)
        a, _, _, pa, _, _ = axes_of(order)
        drain(r3.at[u], ag_two.at[u])
        up, down = along(a, 1), along(a, 3)
        lo, hi = gath.at[u, pl.ds(pa * 16, 8)], gath.at[u, pl.ds(pa * 16 + 8, 8)]
        remote(lo, lo, ag_send.at[2], ag_near.at[u], up).start()
        remote(hi, hi, ag_send.at[2], ag_near.at[u], down).start()
        remote(hi, hi, ag_send.at[2], ag_far.at[u], up).start()
        remote(lo, lo, ag_send.at[2], ag_far.at[u], down).start()

    def ag3(u):
        order, _, _ = place(u, core)
        a, _, _, pa, _, _ = axes_of(order)
        drain(r1.at[u], ag_near.at[u])
        lo, hi = gath.at[u, pl.ds(step(pa, 3) * 16, 8)], gath.at[u, pl.ds(step(pa, 1) * 16 + 8, 8)]
        remote(lo, lo, ag_send.at[3], ag_far.at[u], along(a, 1)).start()
        remote(hi, hi, ag_send.at[3], ag_far.at[u], along(a, 3)).start()

    def strides(order):
        return pick(order, 16, 1, 4), pick(order, 4, 16, 1), pick(order, 1, 4, 16)

    def lay_out(u, source, from_core):
        above = u - tiles
        order, first_row, column = place(u, from_core)
        first_row = first_row - rows_of
        su, sa = strides(order), strides(place(above, from_core)[0])

        def body(yy, carry):
            row = first_row + row_of(1, yy)
            at_u, at_a = yy * su[1], yy * sa[1]
            for zz in range(4):
                for xx in range(4):
                    low = source[u, at_u + xx * su[0] + zz * su[2]].astype(jnp.float32)
                    top = source[above, at_a + xx * sa[0] + zz * sa[2]].astype(jnp.float32)
                    rows = pl.ds(pl.multiple_of(row + xx * shard + zz * 256, half), half)
                    for n in range(2):
                        part = slice(n * rows_of, (n + 1) * rows_of)
                        both = jnp.concatenate([top[part], low[part]], axis=0)
                        out[rows, pl.ds(column + n * lane, lane)] = both.astype(jnp.bfloat16)
            return carry

        lax.fori_loop(0, 4, body, 0)

    def is_lower(u):
        return lax.rem(lax.div(u, tiles), 2) == 1

    def ag4(u):
        drain(r2.at[u], ag_far.at[u])
        remote(gath.at[u], gath_other.at[u], ag_send.at[4], ag_core.at[u], twin).start()

        @pl.when(is_lower(u))
        def _():
            lay_out(u, gath, core)

    def ag5(u):
        drain(gath_other.at[u], ag_core.at[u])

        @pl.when(is_lower(u))
        def _():
            lay_out(u, gath_other, 1 - core)

    for copy in adam_copies:
        copy.wait()
    lead = tiles - 1 + RS[5]
    plan = [(ag5, lead + AG[5]), (ag4, lead + AG[4]), (ag3, lead + AG[3]), (ag2, lead + AG[2]), (ag1, lead + AG[1])]
    plan += [(rs5, RS[5]), (rs4, RS[4]), (rs3, RS[3]), (rs2, RS[2]), (rs1, RS[1]), (rs0, RS[0])]

    plan = plan[::-1]

    def tick(t, carry):
        for work, delay in plan:
            @pl.when(jnp.logical_and(t >= delay, t < delay + units))
            def _(work=work, delay=delay):
                work(t - delay)
        return carry

    lax.fori_loop(0, units + lead + AG[5], tick, 0)

    for n, box in enumerate((peaks_one, peaks_two)):
        drain(box.at[pl.ds(1, (7, 15)[n]), :1], peak_send.at[n])
    drain(other, rs_send.at[0])
    drain(r2, rs_send.at[1])
    drain(r1, rs_send.at[2])
    drain(r3, rs_send.at[3])
    drain(r4, rs_send.at[4])
    drain(r4, ag_send.at[0])
    drain(r3, ag_send.at[1])
    drain(r2, ag_send.at[2])
    drain(r1, ag_send.at[3])
    drain(gath, ag_send.at[4])


def write_back(params, fresh, out, new_master, new_first, new_second, sems):
    parts = 1
    span = blocks // parts
    copies = [pltpu.make_async_copy(fresh.at[n], ref, sems.at[n]) for n, ref in enumerate((new_master, new_first, new_second))]
    for n in range(parts):
        rows = pl.ds(n * span, span)
        copies.append(pltpu.make_async_copy(params.at[rows], out.at[rows], sems.at[3 + n]))
    for copy in copies:
        copy.start()
    for copy in copies:
        copy.wait()


def per_device(gradients, master, first_moment, second_moment):
    bf16, f32 = jnp.bfloat16, jnp.float32
    anywhere = pl.BlockSpec(memory_space=pl.ANY)
    in_vmem = pl.BlockSpec(memory_space=pltpu.VMEM)
    piece = (4, half, lane)
    dma = pltpu.SemaphoreType.DMA
    params, fresh = pl.pallas_call(
        kernel,
        out_shape=(
            pltpu.VMEM((blocks, width), bf16),
            pltpu.VMEM((3, shard, width), f32),
        ),
        in_specs=[anywhere] * 5,
        out_specs=(in_vmem,) * 2,
        scratch_shapes=[
            pltpu.VMEM((blocks, width), f32),
            pltpu.VMEM((rows_of, group), jnp.int32),
            pltpu.VMEM((blocks // 256, 8, width), jnp.int32),
            pltpu.VMEM((group, group), bf16),
            pltpu.VMEM((8, group), f32),
            pltpu.VMEM((8, 8, lane), f32),
            pltpu.VMEM((16, 8, lane), f32),
            pltpu.VMEM((3, shard, width), f32),
            pltpu.VMEM((shard, width), f32),
            pltpu.VMEM((units, 4, 4) + piece, bf16),
            pltpu.VMEM((units, 4, 4) + piece, bf16),
            pltpu.VMEM((units, 4, 4) + piece, bf16),
            pltpu.VMEM((units, 2, 2) + piece, bf16),
            pltpu.VMEM((units, 2, 4) + piece, bf16),
            pltpu.VMEM((units, 4) + piece, bf16),
            pltpu.VMEM((units, 3) + piece, bf16),
            pltpu.VMEM((units,) + piece, bf16),
            pltpu.VMEM((units, 3, half, lane), bf16),
            pltpu.VMEM((units, 64, half, lane), bf16),
            pltpu.VMEM((units, 64, half, lane), bf16),
            dma((chunks,)), dma((1,)), dma((3,)), dma((2,)), dma((2,)),
            dma((5,)), dma((units,)), dma((units,)), dma((units,)), dma((units,)), dma((units,)),
            dma((5,)), dma((units,)), dma((units,)), dma((units,)), dma((units,)), dma((units,)),
        ],
        compiler_params=pltpu.CompilerParams(
            collective_id=0, has_side_effects=True, vmem_limit_bytes=50 * 2**20
        ),
        cost_estimate=pl.CostEstimate(flops=2 * 2**32, bytes_accessed=2**25, transcendentals=0),
        name="reduce_step",
    )(gradients, master, first_moment, second_moment, jnp.asarray(sign_words()))
    params, new_master, new_first, new_second = pl.pallas_call(
        write_back,
        out_shape=(
            jax.ShapeDtypeStruct((blocks, width), bf16),
            jax.ShapeDtypeStruct((shard, width), f32),
            jax.ShapeDtypeStruct((shard, width), f32),
            jax.ShapeDtypeStruct((shard, width), f32),
        ),
        in_specs=[in_vmem] * 2,
        out_specs=(anywhere,) * 4,
        scratch_shapes=[dma((1 + 3,))],
        compiler_params=pltpu.CompilerParams(vmem_limit_bytes=2**20),
        name="write_back",
    )(params, fresh)
    return (new_master, new_first, new_second, params)


def solution(mesh):
    in_specs = (
        P(("inner", "outer"), None, None),
        P(("inner", "outer"), None),
        P(("inner", "outer"), None),
        P(("inner", "outer"), None),
    )
    out_specs = (
        P(("inner", "outer"), None),
        P(("inner", "outer"), None),
        P(("inner", "outer"), None),
        P(),
    )
    return jax.shard_map(
        per_device, mesh=mesh, in_specs=in_specs, out_specs=out_specs, check_vma=False
    )
```

```python
import functools
import math

import jax
import jax.numpy as jnp
import numpy as np
from jax import lax
from jax.experimental import pallas as pl
from jax.experimental.pallas import tpu as pltpu
from jax.sharding import PartitionSpec as P

MESH = pl.DeviceIdType.MESH

code_levels = 127.0
beta_one = 0.9
beta_two = 0.95
learn_rate = 0.002
decay_rate = 0.1
adam_epsilon = 1e-08
first_fix = 1.0 - 0.9**10
second_fix = 1.0 - 0.95**10

blocks = 4096
width = 1024
group = 256
shard = 32
half = 16
lane = 128
rows_of = 8
wide = 2 * lane
tiles = width // wide
units = shard // rows_of * tiles
chunk = 512
chunks = blocks // chunk
sub = 512

hash_one = -1640531535
hash_two = ((-2048144777 << 18) & 0xFFFFFFFF) - (1 << 32 if ((-2048144777 << 18) & 0x80000000) else 0)


def wrap(value):
    value &= 0xFFFFFFFF
    return value - (1 << 32) if value & 0x80000000 else value


RS = (0, 0, 7, 14, 21, 28)
AG = (0, 5, 12, 18, 24, 27)


def sign_words():
    at = np.arange(blocks * width, dtype=np.uint32).reshape(blocks, width)
    hashed = (at * np.uint32(hash_one & 0xFFFFFFFF)).view(np.int32)
    hashed = np.bitwise_xor(hashed, np.right_shift(hashed, 15)).view(np.uint32) * np.uint32(-2048144777 & 0xFFFFFFFF)
    bits = ((hashed >> np.uint32(13)) & np.uint32(1)).reshape(blocks // 256, 32, 8, width)
    return (bits << np.arange(32, dtype=np.uint32)[None, :, None, None]).sum(axis=1, dtype=np.uint32).view(np.int32)


def negative(hashed):
    mixed = jnp.bitwise_xor(hashed, jnp.right_shift(hashed, 15))
    return mixed * jnp.int32(hash_two) < 0


def butterfly(parts):
    p0, p1, p2, p3 = parts
    a, b, c, d = p0 + p1, p0 - p1, p2 + p3, p2 - p3
    return a + c, b + d, a - c, b - d


def pick(order, v0, v1, v2):
    return jnp.where(order == 0, v0, jnp.where(order == 1, v1, v2))


def row_of(axis, v):
    if isinstance(v, int):
        return pick(axis, v * shard, (v % 2) * 128 + (v // 2) * 2048, v * 256)
    return pick(axis, v * shard, lax.rem(v, 2) * 128 + lax.div(v, 2) * 2048, v * 256)


def kernel(
    grad, master, first, second, words,
    out, fresh,
    rot, base, signs, table, peak, peaks_one, peaks_two, adam_in, total,
    other, core_in, s1, r1, r2, t1, r3, t2, r4, gath, gath_other,
    grad_sem, sign_sem, adam_sem, peak_send, peak_recv,
    rs_send, rs_core, rs_one, rs_two, rs_three, rs_four,
    ag_send, ag_one, ag_two, ag_near, ag_far, ag_core,
):
    inner, outer = lax.axis_index("inner"), lax.axis_index("outer")
    core = lax.rem(inner, 2)
    x = lax.rem(outer, 4)
    y = lax.div(inner, 2) * 2 + lax.rem(lax.div(outer, 4), 2)
    z = lax.div(outer, 8)

    def device(xx, yy, zz, cc):
        return (lax.div(yy, 2) * 2 + cc, zz * 8 + lax.rem(yy, 2) * 4 + xx)

    def step(v, d):
        return lax.rem(v + d, 4)

    near = {}
    for d in (1, 2, 3):
        near[0, d] = device(step(x, d), y, z, core)
        near[1, d] = device(x, step(y, d), z, core)
        near[2, d] = device(x, y, step(z, d), core)
    twin = device(x, y, z, 1 - core)

    def along(axis, d):
        return tuple(pick(axis, near[0, d][n], near[1, d][n], near[2, d][n]) for n in (0, 1))

    def remote(src, dst, send, recv, target):
        return pltpu.make_async_remote_copy(
            src_ref=src, dst_ref=dst, send_sem=send, recv_sem=recv, device_id=target, device_id_type=MESH
        )

    def drain(ref, sem):
        pltpu.make_async_copy(ref, ref, sem).wait()

    barrier = pltpu.get_barrier_semaphore()
    column = [device(x, y, step(z, d), c) for d in range(4) for c in (core, 1 - core)][1:]
    plane = [device(step(x, d), step(y, e), z, core) for d in range(4) for e in range(4)][1:]
    partners = column + plane
    for partner in partners:
        pl.semaphore_signal(barrier, inc=1, device_id=partner, device_id_type=MESH)

    def grad_copy(i):
        rows = pl.ds(pl.multiple_of(i * chunk, chunk), chunk)
        return pltpu.make_async_copy(grad.at[0, rows], out.at[rows], grad_sem.at[i])

    def start_grad(i, carry):
        grad_copy(i).start()
        return carry

    sign_copy = pltpu.make_async_copy(words, signs, sign_sem.at[0])
    sign_copy.start()
    lax.fori_loop(0, chunks, start_grad, 0)
    adam_copies = [
        pltpu.make_async_copy(ref, adam_in.at[n], adam_sem.at[n]) for n, ref in enumerate((master, first, second))
    ]
    for copy in adam_copies:
        copy.start()

    rows_i = lax.broadcasted_iota(jnp.int32, (group, group), 0)
    cols_i = lax.broadcasted_iota(jnp.int32, (group, group), 1)
    common = jnp.bitwise_and(rows_i, cols_i)
    for shift in (4, 2, 1):
        common = jnp.bitwise_xor(common, jnp.right_shift(common, shift))
    parity = jnp.bitwise_and(common, 1)
    table[...] = ((1 - 2 * parity).astype(jnp.float32) / math.sqrt(width)).astype(jnp.bfloat16)
    base[...] = (
        lax.broadcasted_iota(jnp.int32, (rows_of, group), 0) * jnp.int32(wrap(width * hash_one))
        + lax.broadcasted_iota(jnp.int32, (rows_of, group), 1) * jnp.int32(hash_one)
    )
    peak[...] = jnp.zeros_like(peak)

    sign_copy.wait()

    def rotate(i, carry):
        grad_copy(i).wait()
        rows = pl.ds(pl.multiple_of(i * sub, sub), sub)
        pieces = []
        for g in range(width // group):
            held = [signs[i * (sub // 256) + n, :, g * group : (g + 1) * group] for n in range(sub // 256)]
            shifted = [jnp.left_shift(word, 31 - r) for word in held for r in range(32)]
            sign = jnp.where(jnp.concatenate(shifted, axis=0) < 0, -1.0, 1.0).astype(jnp.bfloat16)
            flipped = out[rows, g * group : (g + 1) * group] * sign
            pieces.append(flipped)
        turned = jnp.dot(jnp.concatenate(pieces, axis=0), table[...], preferred_element_type=jnp.float32)
        pieces = [turned[g * sub : (g + 1) * sub] for g in range(width // group)]
        top = peak[...]
        for g, piece in enumerate(butterfly(pieces)):
            rot[rows, g * group : (g + 1) * group] = piece
            top = jnp.maximum(top, jnp.max(jnp.abs(piece).reshape(sub // 8, 8, group), axis=0))
        peak[...] = top
        return carry

    lax.fori_loop(0, blocks // sub, rotate, 0)

    pl.semaphore_wait(barrier, len(partners))
    best = jnp.max(jnp.maximum(peak[:, :lane], peak[:, lane:]), axis=0, keepdims=True)
    for n, (stage, box) in enumerate(((column, peaks_one), (plane, peaks_two))):
        box[0, :1] = best
        for k, target in enumerate(stage):
            remote(box.at[0, :1], box.at[1 + k, :1], peak_send.at[n], peak_recv.at[n], target).start()
        arrived = box.at[pl.ds(1, len(stage)), :1]
        drain(arrived, peak_recv.at[n])
        for k in range(len(stage)):
            best = jnp.maximum(best, box[1 + k, :1])
    scale = jnp.max(best)
    ratio = code_levels / (scale + 1e-06)
    decode = (scale + 1e-06) / (code_levels * 128)

    def fold(value):
        return jnp.concatenate([value[:, :lane], value[:, lane:]], axis=0)

    def quantise(row, column):
        value = rot[pl.ds(pl.multiple_of(row, rows_of), rows_of), pl.ds(column, wide)]
        return fold(jnp.floor(value * ratio + 0.5))

    def place(u, owner):
        order = lax.rem(u + owner, 3)
        first_row = owner * 1024 + lax.div(u, tiles) * rows_of
        return order, first_row, pl.multiple_of(lax.rem(u, tiles) * wide, wide)

    def axes_of(order):
        a, b, c = order, lax.rem(order + 1, 3), lax.rem(order + 2, 3)
        return a, b, c, pick(a, x, y, z), pick(b, x, y, z), pick(c, x, y, z)

    def each_tile(order, first_row, work):
        a, b, c = order, lax.rem(order + 1, 3), lax.rem(order + 2, 3)
        in_b = [row_of(b, j) for j in range(4)]
        in_c = [row_of(c, k) for k in range(4)]

        def body(i, carry):
            start = first_row + row_of(a, i)
            for j in range(4):
                for k in range(4):
                    work(i, j, k, start + in_b[j] + in_c[k])
            return carry

        lax.fori_loop(0, 4, body, 0)

    def rs0(u):
        order, first_row, column = place(u, 1 - core)

        def work(i, j, k, row):
            other[u, i, j, k] = quantise(row, column).astype(jnp.bfloat16)

        each_tile(order, first_row, work)
        remote(other.at[u], core_in.at[u], rs_send.at[0], rs_core.at[u], twin).start()

    def rs1(u):
        order, first_row, column = place(u, core)
        drain(core_in.at[u], rs_core.at[u])

        def work(i, j, k, row):
            mine = quantise(row, column)
            s1[u, i, j, k] = (mine + core_in[u, i, j, k].astype(jnp.float32)).astype(jnp.bfloat16)

        each_tile(order, first_row, work)
        a, _, _, pa, _, _ = axes_of(order)
        up, down = along(a, 1), along(a, 3)
        far = step(pa, 2)
        lo, hi = pl.ds(0, 2), pl.ds(2, 2)
        remote(s1.at[u, far, lo], r1.at[u, 0], rs_send.at[1], rs_one.at[u], up).start()
        remote(s1.at[u, far, hi], r1.at[u, 1], rs_send.at[1], rs_one.at[u], down).start()

    def rs2(u):
        order, _, _ = place(u, core)
        a, _, _, pa, _, _ = axes_of(order)
        pu, pd = step(pa, 1), step(pa, 3)
        lo, hi = pl.ds(0, 2), pl.ds(2, 2)
        drain(r1.at[u], rs_one.at[u])
        s1[u, pu, lo] += r1[u, 0]
        s1[u, pd, hi] += r1[u, 1]
        remote(s1.at[u, pu], r2.at[u, 0], rs_send.at[2], rs_two.at[u], along(a, 1)).start()
        remote(s1.at[u, pd], r2.at[u, 1], rs_send.at[2], rs_two.at[u], along(a, 3)).start()

    def rs3(u):
        order, _, _ = place(u, core)
        _, b, _, pa, pb, _ = axes_of(order)
        drain(r2.at[u], rs_two.at[u])
        f32 = jnp.float32
        t1[u] = (s1[u, pa].astype(f32) + r2[u, 0].astype(f32) + r2[u, 1].astype(f32)).astype(jnp.bfloat16)
        for n, d in enumerate((1, 3, 2)):
            remote(t1.at[u, step(pb, d)], r3.at[u, n], rs_send.at[3], rs_three.at[u], along(b, d)).start()

    def rs4(u):
        order, _, _ = place(u, core)
        _, _, c, _, pb, pc = axes_of(order)
        drain(r3.at[u], rs_three.at[u])
        f32 = jnp.float32
        t2[u] = (
            t1[u, pb].astype(f32) + r3[u, 0].astype(f32) + r3[u, 1].astype(f32) + r3[u, 2].astype(f32)
        ).astype(jnp.bfloat16)
        for n, d in enumerate((1, 3, 2)):
            remote(t2.at[u, step(pc, d)], r4.at[u, n], rs_send.at[4], rs_four.at[u], along(c, d)).start()

    def rs5(u):
        order, _, column = place(u, core)
        pc = axes_of(order)[5]
        drain(r4.at[u], rs_four.at[u])
        f32 = jnp.float32
        value = t2[u, pc].astype(f32) + r4[u, 0].astype(f32) + r4[u, 1].astype(f32) + r4[u, 2].astype(f32)
        rows = pl.ds(pl.multiple_of(lax.div(u, tiles) * rows_of, rows_of), rows_of)
        total[rows, pl.ds(column, lane)] = value[:rows_of]
        total[rows, pl.ds(column + lane, lane)] = value[rows_of:]

        @pl.when(lax.rem(u, tiles) == tiles - 1)
        def _():
            update(lax.div(u, tiles))

    owner = inner * 32 + outer

    def update(h):
        rows = pl.ds(pl.multiple_of(h * rows_of, rows_of), rows_of)
        value = jnp.concatenate([total[rows, g * group : (g + 1) * group] for g in range(width // group)], axis=0)
        high = jnp.floor(value * (1.0 / 128.0) + 0.5)
        stacked = jnp.concatenate([high, value - high * 128.0], axis=0).astype(jnp.bfloat16)
        product = jnp.dot(stacked, table[...], preferred_element_type=jnp.float32)
        product = product[: 4 * rows_of] * 128.0 + product[4 * rows_of :]
        parts = [product[g * rows_of : (g + 1) * rows_of] for g in range(width // group)]
        for g, turned in enumerate(butterfly(parts)):
            columns = slice(g * group, (g + 1) * group)
            offset = (owner * shard + h * rows_of) * jnp.int32(wrap(width * hash_one)) + jnp.int32(wrap(g * group * hash_one))
            mean = turned * decode
            mean = jnp.where(negative(base[...] + offset), -mean, mean)
            one = beta_one * adam_in[1, rows, columns] + (1.0 - beta_one) * mean
            two = beta_two * adam_in[2, rows, columns] + (1.0 - beta_two) * mean * mean
            old = adam_in[0, rows, columns]
            size = one / first_fix / (jnp.sqrt(two / second_fix) + adam_epsilon)
            new = old - learn_rate * (size + decay_rate * old)
            fresh[1, rows, columns] = one
            fresh[2, rows, columns] = two
            fresh[0, rows, columns] = new
            u = h * tiles + g
            order, _, _ = place(u, core)
            _, _, c, pa, pb, pc = axes_of(order)
            mine = pa * 16 + pb * 4 + pc
            gath[u, mine] = fold(new).astype(jnp.bfloat16)
            for d in (1, 3, 2):
                remote(gath.at[u, mine], gath.at[u, mine], ag_send.at[0], ag_one.at[u], along(c, d)).start()

    def ag1(u):
        order, _, _ = place(u, core)
        _, b, _, pa, pb, _ = axes_of(order)
        drain(r4.at[u], ag_one.at[u])
        row = gath.at[u, pl.ds(pa * 16 + pb * 4, 4)]
        for d in (1, 3, 2):
            remote(row, row, ag_send.at[1], ag_two.at[u], along(b, d)).start()

    def ag2(u):
        order, _, _ = place(u, core)
        a, _, _, pa, _, _ = axes_of(order)
        drain(r3.at[u], ag_two.at[u])
        up, down = along(a, 1), along(a, 3)
        lo, hi = gath.at[u, pl.ds(pa * 16, 8)], gath.at[u, pl.ds(pa * 16 + 8, 8)]
        remote(lo, lo, ag_send.at[2], ag_near.at[u], up).start()
        remote(hi, hi, ag_send.at[2], ag_near.at[u], down).start()

    def ag3(u):
        order, _, _ = place(u, core)
        a, _, _, pa, _, _ = axes_of(order)
        drain(r1.at[u], ag_near.at[u])
        lo, hi = gath.at[u, pl.ds(step(pa, 3) * 16, 8)], gath.at[u, pl.ds(step(pa, 1) * 16 + 8, 8)]
        up, down = along(a, 1), along(a, 3)
        remote(lo, lo, ag_send.at[3], ag_far.at[u], up).start()
        remote(hi, hi, ag_send.at[3], ag_far.at[u], down).start()
        lo, hi = gath.at[u, pl.ds(pa * 16, 8)], gath.at[u, pl.ds(pa * 16 + 8, 8)]
        remote(hi, hi, ag_send.at[3], ag_far.at[u], up).start()
        remote(lo, lo, ag_send.at[3], ag_far.at[u], down).start()

    def strides(order):
        return pick(order, 16, 1, 4), pick(order, 4, 16, 1), pick(order, 1, 4, 16)

    def lay_out(u, source, from_core):
        above = u - tiles
        order, first_row, column = place(u, from_core)
        first_row = first_row - rows_of
        su, sa = strides(order), strides(place(above, from_core)[0])

        def body(yy, carry):
            row = first_row + row_of(1, yy)
            at_u, at_a = yy * su[1], yy * sa[1]
            for zz in range(4):
                for xx in range(4):
                    low = source[u, at_u + xx * su[0] + zz * su[2]].astype(jnp.float32)
                    top = source[above, at_a + xx * sa[0] + zz * sa[2]].astype(jnp.float32)
                    rows = pl.ds(pl.multiple_of(row + xx * shard + zz * 256, half), half)
                    for n in range(2):
                        part = slice(n * rows_of, (n + 1) * rows_of)
                        both = jnp.concatenate([top[part], low[part]], axis=0)
                        out[rows, pl.ds(column + n * lane, lane)] = both.astype(jnp.bfloat16)
            return carry

        lax.fori_loop(0, 4, body, 0)

    def is_lower(u):
        return lax.rem(lax.div(u, tiles), 2) == 1

    def ag4(u):
        drain(r2.at[u], ag_far.at[u])
        remote(gath.at[u], gath_other.at[u], ag_send.at[4], ag_core.at[u], twin).start()

        @pl.when(is_lower(u))
        def _():
            lay_out(u, gath, core)

    def ag5(u):
        drain(gath_other.at[u], ag_core.at[u])

        @pl.when(is_lower(u))
        def _():
            lay_out(u, gath_other, 1 - core)

    for copy in adam_copies:
        copy.wait()
    lead = tiles - 1 + RS[5]
    plan = [(rs1, RS[1]), (rs2, RS[2]), (rs3, RS[3]), (rs4, RS[4]), (rs5, RS[5])]
    plan += [(ag1, lead + AG[1]), (ag2, lead + AG[2]), (ag3, lead + AG[3]), (ag4, lead + AG[4]), (ag5, lead + AG[5])]

    def first_step(u, carry):
        rs0(u)
        return carry

    lax.fori_loop(0, units, first_step, 0)

    marks = sorted({delay for _, delay in plan} | {delay + units for _, delay in plan})
    for begin, end in zip(marks, marks[1:]):
        running = [(work, delay) for work, delay in plan if delay <= begin and end <= delay + units]

        def tick(t, carry, running=running):
            for work, delay in running:
                work(t - delay)
            return carry

        lax.fori_loop(begin, end, tick, 0)

    for n, box in enumerate((peaks_one, peaks_two)):
        drain(box.at[pl.ds(1, (7, 15)[n]), :1], peak_send.at[n])
    drain(other, rs_send.at[0])
    drain(r1, rs_send.at[1])
    drain(r2, rs_send.at[2])
    drain(r3, rs_send.at[3])
    drain(r4, rs_send.at[4])
    drain(r4, ag_send.at[0])
    drain(r3, ag_send.at[1])
    drain(r1, ag_send.at[2])
    drain(r2, ag_send.at[3])
    drain(gath, ag_send.at[4])


def write_back(params, fresh, out, new_master, new_first, new_second, sems):
    parts = 1
    span = blocks // parts
    copies = [pltpu.make_async_copy(fresh.at[n], ref, sems.at[n]) for n, ref in enumerate((new_master, new_first, new_second))]
    for n in range(parts):
        rows = pl.ds(n * span, span)
        copies.append(pltpu.make_async_copy(params.at[rows], out.at[rows], sems.at[3 + n]))
    for copy in copies:
        copy.start()
    for copy in copies:
        copy.wait()


def per_device(gradients, master, first_moment, second_moment):
    bf16, f32 = jnp.bfloat16, jnp.float32
    anywhere = pl.BlockSpec(memory_space=pl.ANY)
    in_vmem = pl.BlockSpec(memory_space=pltpu.VMEM)
    piece = (4, half, lane)
    dma = pltpu.SemaphoreType.DMA
    params, fresh = pl.pallas_call(
        kernel,
        out_shape=(
            pltpu.VMEM((blocks, width), bf16),
            pltpu.VMEM((3, shard, width), f32),
        ),
        in_specs=[anywhere] * 5,
        out_specs=(in_vmem,) * 2,
        scratch_shapes=[
            pltpu.VMEM((blocks, width), f32),
            pltpu.VMEM((rows_of, group), jnp.int32),
            pltpu.VMEM((blocks // 256, 8, width), jnp.int32),
            pltpu.VMEM((group, group), bf16),
            pltpu.VMEM((8, group), f32),
            pltpu.VMEM((8, 8, lane), f32),
            pltpu.VMEM((16, 8, lane), f32),
            pltpu.VMEM((3, shard, width), f32),
            pltpu.VMEM((shard, width), f32),
            pltpu.VMEM((units, 4, 4) + piece, bf16),
            pltpu.VMEM((units, 4, 4) + piece, bf16),
            pltpu.VMEM((units, 4, 4) + piece, bf16),
            pltpu.VMEM((units, 2, 2) + piece, bf16),
            pltpu.VMEM((units, 2, 4) + piece, bf16),
            pltpu.VMEM((units, 4) + piece, bf16),
            pltpu.VMEM((units, 3) + piece, bf16),
            pltpu.VMEM((units,) + piece, bf16),
            pltpu.VMEM((units, 3, half, lane), bf16),
            pltpu.VMEM((units, 64, half, lane), bf16),
            pltpu.VMEM((units, 64, half, lane), bf16),
            dma((chunks,)), dma((1,)), dma((3,)), dma((2,)), dma((2,)),
            dma((5,)), dma((units,)), dma((units,)), dma((units,)), dma((units,)), dma((units,)),
            dma((5,)), dma((units,)), dma((units,)), dma((units,)), dma((units,)), dma((units,)),
        ],
        compiler_params=pltpu.CompilerParams(
            collective_id=0, has_side_effects=True, vmem_limit_bytes=50 * 2**20
        ),
        cost_estimate=pl.CostEstimate(flops=2 * 2**32, bytes_accessed=2**25, transcendentals=0),
        name="reduce_step",
    )(gradients, master, first_moment, second_moment, jnp.asarray(sign_words()))
    params, new_master, new_first, new_second = pl.pallas_call(
        write_back,
        out_shape=(
            jax.ShapeDtypeStruct((blocks, width), bf16),
            jax.ShapeDtypeStruct((shard, width), f32),
            jax.ShapeDtypeStruct((shard, width), f32),
            jax.ShapeDtypeStruct((shard, width), f32),
        ),
        in_specs=[in_vmem] * 2,
        out_specs=(anywhere,) * 4,
        scratch_shapes=[dma((1 + 3,))],
        compiler_params=pltpu.CompilerParams(vmem_limit_bytes=2**20),
        name="write_back",
    )(params, fresh)
    return (new_master, new_first, new_second, params)


def solution(mesh):
    in_specs = (
        P(("inner", "outer"), None, None),
        P(("inner", "outer"), None),
        P(("inner", "outer"), None),
        P(("inner", "outer"), None),
    )
    out_specs = (
        P(("inner", "outer"), None),
        P(("inner", "outer"), None),
        P(("inner", "outer"), None),
        P(),
    )
    return jax.shard_map(
        per_device, mesh=mesh, in_specs=in_specs, out_specs=out_specs, check_vma=False
    )
```

```python
import functools
import math

import jax
import jax.numpy as jnp
import numpy as np
from jax import lax
from jax.experimental import pallas as pl
from jax.experimental.pallas import tpu as pltpu
from jax.sharding import PartitionSpec as P

MESH = pl.DeviceIdType.MESH

code_levels = 127.0
beta_one = 0.9
beta_two = 0.95
learn_rate = 0.002
decay_rate = 0.1
adam_epsilon = 1e-08
first_fix = 1.0 - 0.9**10
second_fix = 1.0 - 0.95**10

blocks = 4096
width = 1024
group = 256
shard = 32
half = 16
lane = 128
rows_of = 8
wide = 2 * lane
tiles = width // wide
units = shard // rows_of * tiles
early = tiles
chunk = 512
chunks = blocks // chunk
sub = 512

hash_one = -1640531535
hash_two = ((-2048144777 << 18) & 0xFFFFFFFF) - (1 << 32 if ((-2048144777 << 18) & 0x80000000) else 0)


def wrap(value):
    value &= 0xFFFFFFFF
    return value - (1 << 32) if value & 0x80000000 else value


RS = (0, 0, 7, 14, 22, 29)
AG = (0, 6, 13, 19, 26, 30)


def sign_words():
    at = np.arange(blocks * width, dtype=np.uint32).reshape(blocks, width)
    hashed = (at * np.uint32(hash_one & 0xFFFFFFFF)).view(np.int32)
    hashed = np.bitwise_xor(hashed, np.right_shift(hashed, 15)).view(np.uint32) * np.uint32(-2048144777 & 0xFFFFFFFF)
    bits = ((hashed >> np.uint32(13)) & np.uint32(1)).reshape(blocks // 256, 32, 8, width)
    return (bits << np.arange(32, dtype=np.uint32)[None, :, None, None]).sum(axis=1, dtype=np.uint32).view(np.int32)


def negative(hashed):
    mixed = jnp.bitwise_xor(hashed, jnp.right_shift(hashed, 15))
    return mixed * jnp.int32(hash_two) < 0


def butterfly(parts):
    p0, p1, p2, p3 = parts
    a, b, c, d = p0 + p1, p0 - p1, p2 + p3, p2 - p3
    return a + c, b + d, a - c, b - d


def pick(order, v0, v1, v2):
    return jnp.where(order == 0, v0, jnp.where(order == 1, v1, v2))


def shard_of(axis, v):
    if isinstance(v, int):
        return pick(axis, v, (v % 2) * 4 + (v // 2) * 64, v * 8)
    return pick(axis, v, lax.rem(v, 2) * 4 + lax.div(v, 2) * 64, v * 8)


def kernel(
    grad, master, first, second, words,
    out, fresh,
    rot, twin_rot, base, signs, table, peak, peaks_one, peaks_two, adam_in, total,
    other, core_in, s1, r1, r2, t1, r3, t2, r4, gath, gath_other,
    grad_sem, sign_sem, twin_send, twin_recv, adam_sem, peak_send, peak_recv,
    rs_send, rs_core, rs_one, rs_two, rs_three, rs_four,
    ag_send, ag_one, ag_two, ag_near, ag_far, ag_core,
):
    inner, outer = lax.axis_index("inner"), lax.axis_index("outer")
    core = lax.rem(inner, 2)
    x = lax.rem(outer, 4)
    y = lax.div(inner, 2) * 2 + lax.rem(lax.div(outer, 4), 2)
    z = lax.div(outer, 8)

    def device(xx, yy, zz, cc):
        return (lax.div(yy, 2) * 2 + cc, zz * 8 + lax.rem(yy, 2) * 4 + xx)

    def step(v, d):
        return lax.rem(v + d, 4)

    near = {}
    for d in (1, 2, 3):
        near[0, d] = device(step(x, d), y, z, core)
        near[1, d] = device(x, step(y, d), z, core)
        near[2, d] = device(x, y, step(z, d), core)
    twin = device(x, y, z, 1 - core)

    def along(axis, d):
        return tuple(pick(axis, near[0, d][n], near[1, d][n], near[2, d][n]) for n in (0, 1))

    def remote(src, dst, send, recv, target):
        return pltpu.make_async_remote_copy(
            src_ref=src, dst_ref=dst, send_sem=send, recv_sem=recv, device_id=target, device_id_type=MESH
        )

    def drain(ref, sem):
        pltpu.make_async_copy(ref, ref, sem).wait()

    barrier = pltpu.get_barrier_semaphore()
    column = [device(x, y, step(z, d), c) for d in range(4) for c in (core, 1 - core)][1:]
    plane = [device(step(x, d), step(y, e), z, core) for d in range(4) for e in range(4)][1:]
    partners = column + plane
    for partner in partners:
        pl.semaphore_signal(barrier, inc=1, device_id=partner, device_id_type=MESH)

    def grad_copy(i):
        rows = pl.ds(pl.multiple_of(i * chunk, chunk), chunk)
        return pltpu.make_async_copy(grad.at[0, rows], out.at[rows], grad_sem.at[i])

    def start_grad(i, carry):
        grad_copy(i).start()
        return carry

    sign_copy = pltpu.make_async_copy(words, signs, sign_sem.at[0])
    sign_copy.start()
    lax.fori_loop(0, chunks, start_grad, 0)
    adam_copies = [
        pltpu.make_async_copy(ref, adam_in.at[n], adam_sem.at[n]) for n, ref in enumerate((master, first, second))
    ]
    for copy in adam_copies:
        copy.start()

    rows_i = lax.broadcasted_iota(jnp.int32, (group, group), 0)
    cols_i = lax.broadcasted_iota(jnp.int32, (group, group), 1)
    common = jnp.bitwise_and(rows_i, cols_i)
    for shift in (4, 2, 1):
        common = jnp.bitwise_xor(common, jnp.right_shift(common, shift))
    parity = jnp.bitwise_and(common, 1)
    table[...] = ((1 - 2 * parity).astype(jnp.float32) / math.sqrt(width)).astype(jnp.bfloat16)
    base[...] = (
        lax.broadcasted_iota(jnp.int32, (rows_of, group), 0) * jnp.int32(wrap(width * hash_one))
        + lax.broadcasted_iota(jnp.int32, (rows_of, group), 1) * jnp.int32(hash_one)
    )
    peak[...] = jnp.zeros_like(peak)

    sign_copy.wait()

    def rotate(i, carry):
        grad_copy(i).wait()
        rows = pl.ds(pl.multiple_of(i * sub, sub), sub)
        pieces = []
        for g in range(width // group):
            held = [signs[i * (sub // 256) + n, :, g * group : (g + 1) * group] for n in range(sub // 256)]
            shifted = [jnp.left_shift(word, 31 - r) for word in held for r in range(32)]
            sign = jnp.where(jnp.concatenate(shifted, axis=0) < 0, -1.0, 1.0).astype(jnp.bfloat16)
            flipped = out[rows, g * group : (g + 1) * group] * sign
            pieces.append(flipped)
        turned = jnp.dot(jnp.concatenate(pieces, axis=0), table[...], preferred_element_type=jnp.float32)
        pieces = [turned[g * sub : (g + 1) * sub] for g in range(width // group)]
        top = peak[...]
        for g, piece in enumerate(butterfly(pieces)):
            held = pl.ds(pl.multiple_of(i * (sub // shard), sub // shard), sub // shard)
            rot[held, :, g * group : (g + 1) * group] = piece.reshape(sub // shard, shard, group)
            top = jnp.maximum(top, jnp.max(jnp.abs(piece).reshape(sub // 8, 8, group), axis=0))
        peak[...] = top
        return carry

    lax.fori_loop(0, blocks // sub, rotate, 0)

    pl.semaphore_wait(barrier, len(partners))
    best = jnp.max(jnp.maximum(peak[:, :lane], peak[:, lane:]), axis=0, keepdims=True)
    twin_copies = []
    for n in range(2):
        span = pl.ds(pl.multiple_of(n * 64 + (1 - core) * 32, 32), 32)
        twin_copies.append(
            remote(rot.at[span, pl.ds(0, rows_of)], twin_rot.at[span], twin_send.at[n], twin_recv.at[n], twin)
        )
    for n, (stage, box) in enumerate(((column, peaks_one), (plane, peaks_two))):
        box[0, :1] = best
        for k, target in enumerate(stage):
            remote(box.at[0, :1], box.at[1 + k, :1], peak_send.at[n], peak_recv.at[n], target).start()
        if n == 0:
            for copy in twin_copies:
                copy.start()
        arrived = box.at[pl.ds(1, len(stage)), :1]
        drain(arrived, peak_recv.at[n])
        for k in range(len(stage)):
            best = jnp.maximum(best, box[1 + k, :1])
    scale = jnp.max(best)
    ratio = code_levels / (scale + 1e-06)
    decode = (scale + 1e-06) / (code_levels * 128)

    def fold(value):
        return jnp.concatenate([value[:, :lane], value[:, lane:]], axis=0)

    def quantise(owned, row, column):
        value = rot[owned, pl.ds(row, rows_of), pl.ds(column, wide)]
        return fold(jnp.floor(value * ratio + 0.5))

    def quantise_twin(owned, column):
        value = twin_rot[owned, :, pl.ds(column, wide)]
        return fold(jnp.floor(value * ratio + 0.5))

    def place(u, owner):
        order = lax.rem(u + owner, 3)
        first_row = owner * 1024 + lax.div(u, tiles) * rows_of
        return order, first_row, pl.multiple_of(lax.rem(u, tiles) * wide, wide)

    def axes_of(order):
        a, b, c = order, lax.rem(order + 1, 3), lax.rem(order + 2, 3)
        return a, b, c, pick(a, x, y, z), pick(b, x, y, z), pick(c, x, y, z)

    def each_tile(order, first, work):
        a, b, c = order, lax.rem(order + 1, 3), lax.rem(order + 2, 3)
        in_b = [shard_of(b, j) for j in range(4)]
        in_c = [shard_of(c, k) for k in range(4)]

        def body(i, carry):
            start = first + shard_of(a, i)
            for j in range(4):
                for k in range(4):
                    work(i, j, k, start + in_b[j] + in_c[k])
            return carry

        lax.fori_loop(0, 4, body, 0)

    def row_in(u):
        return pl.multiple_of(lax.div(u, tiles) * rows_of, rows_of)

    def rs0(u):
        order, _, column = place(u, 1 - core)
        row = row_in(u)

        def work(i, j, k, owned):
            other[u, i, j, k] = quantise(owned, row, column).astype(jnp.bfloat16)

        each_tile(order, 32 * (1 - core), work)
        remote(other.at[u], core_in.at[u], rs_send.at[0], rs_core.at[u], twin).start()

    def rs1_early(u):
        order, _, column = place(u, core)
        row = row_in(u)

        def work(i, j, k, owned):
            s1[u, i, j, k] = (quantise(owned, row, column) + quantise_twin(owned, column)).astype(jnp.bfloat16)

        each_tile(order, 32 * core, work)
        send_far(u, order)

    def rs1(u):
        order, _, column = place(u, core)
        row = row_in(u)
        drain(core_in.at[u], rs_core.at[u])

        def work(i, j, k, owned):
            mine = quantise(owned, row, column)
            s1[u, i, j, k] = (mine + core_in[u, i, j, k].astype(jnp.float32)).astype(jnp.bfloat16)

        each_tile(order, 32 * core, work)
        send_far(u, order)

    def send_far(u, order):
        a, _, _, pa, _, _ = axes_of(order)
        up, down = along(a, 1), along(a, 3)
        far = step(pa, 2)
        lo, hi = pl.ds(0, 2), pl.ds(2, 2)
        remote(s1.at[u, far, lo], r1.at[u, 0], rs_send.at[1], rs_one.at[u], up).start()
        remote(s1.at[u, far, hi], r1.at[u, 1], rs_send.at[1], rs_one.at[u], down).start()

    def rs2(u):
        order, _, _ = place(u, core)
        a, _, _, pa, _, _ = axes_of(order)
        pu, pd = step(pa, 1), step(pa, 3)
        lo, hi = pl.ds(0, 2), pl.ds(2, 2)
        drain(r1.at[u], rs_one.at[u])
        s1[u, pu, lo] += r1[u, 0]
        s1[u, pd, hi] += r1[u, 1]
        remote(s1.at[u, pu], r2.at[u, 0], rs_send.at[2], rs_two.at[u], along(a, 1)).start()
        remote(s1.at[u, pd], r2.at[u, 1], rs_send.at[2], rs_two.at[u], along(a, 3)).start()

    def rs3(u):
        order, _, _ = place(u, core)
        _, b, _, pa, pb, _ = axes_of(order)
        drain(r2.at[u], rs_two.at[u])
        f32 = jnp.float32
        t1[u] = (s1[u, pa].astype(f32) + r2[u, 0].astype(f32) + r2[u, 1].astype(f32)).astype(jnp.bfloat16)
        for n, d in enumerate((1, 3, 2)):
            remote(t1.at[u, step(pb, d)], r3.at[u, n], rs_send.at[3], rs_three.at[u], along(b, d)).start()

    def rs4(u):
        order, _, _ = place(u, core)
        _, _, c, _, pb, pc = axes_of(order)
        drain(r3.at[u], rs_three.at[u])
        f32 = jnp.float32
        t2[u] = (
            t1[u, pb].astype(f32) + r3[u, 0].astype(f32) + r3[u, 1].astype(f32) + r3[u, 2].astype(f32)
        ).astype(jnp.bfloat16)
        for n, d in enumerate((1, 3, 2)):
            remote(t2.at[u, step(pc, d)], r4.at[u, n], rs_send.at[4], rs_four.at[u], along(c, d)).start()

    def rs5(u):
        order, _, column = place(u, core)
        pc = axes_of(order)[5]
        drain(r4.at[u], rs_four.at[u])
        f32 = jnp.float32
        value = t2[u, pc].astype(f32) + r4[u, 0].astype(f32) + r4[u, 1].astype(f32) + r4[u, 2].astype(f32)
        rows = pl.ds(pl.multiple_of(lax.div(u, tiles) * rows_of, rows_of), rows_of)
        total[rows, pl.ds(column, lane)] = value[:rows_of]
        total[rows, pl.ds(column + lane, lane)] = value[rows_of:]

        @pl.when(lax.rem(u, tiles) == tiles - 1)
        def _():
            update(lax.div(u, tiles))

    owner = inner * 32 + outer

    def update(h):
        rows = pl.ds(pl.multiple_of(h * rows_of, rows_of), rows_of)
        value = jnp.concatenate([total[rows, g * group : (g + 1) * group] for g in range(width // group)], axis=0)
        high = jnp.floor(value * (1.0 / 128.0) + 0.5)
        stacked = jnp.concatenate([high, value - high * 128.0], axis=0).astype(jnp.bfloat16)
        product = jnp.dot(stacked, table[...], preferred_element_type=jnp.float32)
        product = product[: 4 * rows_of] * 128.0 + product[4 * rows_of :]
        parts = [product[g * rows_of : (g + 1) * rows_of] for g in range(width // group)]
        for g, turned in enumerate(butterfly(parts)):
            columns = slice(g * group, (g + 1) * group)
            offset = (owner * shard + h * rows_of) * jnp.int32(wrap(width * hash_one)) + jnp.int32(wrap(g * group * hash_one))
            mean = turned * decode
            mean = jnp.where(negative(base[...] + offset), -mean, mean)
            one = beta_one * adam_in[1, rows, columns] + (1.0 - beta_one) * mean
            two = beta_two * adam_in[2, rows, columns] + (1.0 - beta_two) * mean * mean
            old = adam_in[0, rows, columns]
            size = one / first_fix / (jnp.sqrt(two / second_fix) + adam_epsilon)
            new = old - learn_rate * (size + decay_rate * old)
            fresh[1, rows, columns] = one
            fresh[2, rows, columns] = two
            fresh[0, rows, columns] = new
            u = h * tiles + g
            order, _, _ = place(u, core)
            _, _, c, pa, pb, pc = axes_of(order)
            mine = pa * 16 + pb * 4 + pc
            gath[u, mine] = fold(new).astype(jnp.bfloat16)
            for d in (1, 3, 2):
                remote(gath.at[u, mine], gath.at[u, mine], ag_send.at[0], ag_one.at[u], along(c, d)).start()

    def ag1(u):
        order, _, _ = place(u, core)
        _, b, _, pa, pb, _ = axes_of(order)
        drain(r4.at[u], ag_one.at[u])
        row = gath.at[u, pl.ds(pa * 16 + pb * 4, 4)]
        for d in (1, 3, 2):
            remote(row, row, ag_send.at[1], ag_two.at[u], along(b, d)).start()

    def ag2(u):
        order, _, _ = place(u, core)
        a, _, _, pa, _, _ = axes_of(order)
        drain(r3.at[u], ag_two.at[u])
        up, down = along(a, 1), along(a, 3)
        lo, hi = gath.at[u, pl.ds(pa * 16, 8)], gath.at[u, pl.ds(pa * 16 + 8, 8)]
        remote(lo, lo, ag_send.at[2], ag_near.at[u], up).start()
        remote(hi, hi, ag_send.at[2], ag_near.at[u], down).start()

    def ag3(u):
        order, _, _ = place(u, core)
        a, _, _, pa, _, _ = axes_of(order)
        drain(r1.at[u], ag_near.at[u])
        lo, hi = gath.at[u, pl.ds(step(pa, 3) * 16, 8)], gath.at[u, pl.ds(step(pa, 1) * 16 + 8, 8)]
        up, down = along(a, 1), along(a, 3)
        remote(lo, lo, ag_send.at[3], ag_far.at[u], up).start()
        remote(hi, hi, ag_send.at[3], ag_far.at[u], down).start()
        lo, hi = gath.at[u, pl.ds(pa * 16, 8)], gath.at[u, pl.ds(pa * 16 + 8, 8)]
        remote(hi, hi, ag_send.at[3], ag_far.at[u], up).start()
        remote(lo, lo, ag_send.at[3], ag_far.at[u], down).start()

    def strides(order):
        return pick(order, 16, 1, 4), pick(order, 4, 16, 1), pick(order, 1, 4, 16)

    def lay_out(u, source, from_core):
        above = u - tiles
        order, first_row, column = place(u, from_core)
        first_row = first_row - rows_of
        su, sa = strides(order), strides(place(above, from_core)[0])

        def body(yy, carry):
            row = first_row + shard_of(1, yy) * shard
            at_u, at_a = yy * su[1], yy * sa[1]
            for zz in range(4):
                for xx in range(4):
                    low = source[u, at_u + xx * su[0] + zz * su[2]].astype(jnp.float32)
                    top = source[above, at_a + xx * sa[0] + zz * sa[2]].astype(jnp.float32)
                    rows = pl.ds(pl.multiple_of(row + xx * shard + zz * 256, half), half)
                    for n in range(2):
                        part = slice(n * rows_of, (n + 1) * rows_of)
                        both = jnp.concatenate([top[part], low[part]], axis=0)
                        out[rows, pl.ds(column + n * lane, lane)] = both.astype(jnp.bfloat16)
            return carry

        lax.fori_loop(0, 4, body, 0)

    def is_lower(u):
        return lax.rem(lax.div(u, tiles), 2) == 1

    def ag4(u):
        drain(r2.at[u], ag_far.at[u])
        remote(gath.at[u], gath_other.at[u], ag_send.at[4], ag_core.at[u], twin).start()

        @pl.when(is_lower(u))
        def _():
            lay_out(u, gath, core)

    def ag5(u):
        drain(gath_other.at[u], ag_core.at[u])

        @pl.when(is_lower(u))
        def _():
            lay_out(u, gath_other, 1 - core)

    for copy in adam_copies:
        copy.wait()
    lead = tiles - 1 + RS[5]
    plan = [(rs1, RS[1], early), (rs2, RS[2], 0), (rs3, RS[3], 0), (rs4, RS[4], 0), (rs5, RS[5], 0)]
    plan += [(work, lead + AG[n + 1], 0) for n, work in enumerate((ag1, ag2, ag3, ag4, ag5))]
    for copy in twin_copies:
        copy.wait_recv()

    def repeat(work, begin, end):
        def body(u, carry):
            work(u)
            return carry

        lax.fori_loop(begin, end, body, 0)

    repeat(rs1_early, 0, early)
    repeat(rs0, early, units)

    marks = sorted({delay + first for _, delay, first in plan} | {delay + units for _, delay, _ in plan})
    for begin, end in zip(marks, marks[1:]):
        running = [(work, delay) for work, delay, first in plan if delay + first <= begin and end <= delay + units]

        def tick(t, running=running):
            for work, delay in running:
                work(t - delay)

        repeat(tick, begin, end)

    for copy in twin_copies:
        copy.wait_send()
    for n, box in enumerate((peaks_one, peaks_two)):
        drain(box.at[pl.ds(1, (7, 15)[n]), :1], peak_send.at[n])
    drain(other.at[pl.ds(early, units - early)], rs_send.at[0])
    drain(r1, rs_send.at[1])
    drain(r2, rs_send.at[2])
    drain(r3, rs_send.at[3])
    drain(r4, rs_send.at[4])
    drain(r4, ag_send.at[0])
    drain(r3, ag_send.at[1])
    drain(r1, ag_send.at[2])
    drain(r2, ag_send.at[3])
    drain(gath, ag_send.at[4])


def write_back(params, fresh, out, new_master, new_first, new_second, sems):
    parts = 1
    span = blocks // parts
    copies = [pltpu.make_async_copy(fresh.at[n], ref, sems.at[n]) for n, ref in enumerate((new_master, new_first, new_second))]
    for n in range(parts):
        rows = pl.ds(n * span, span)
        copies.append(pltpu.make_async_copy(params.at[rows], out.at[rows], sems.at[3 + n]))
    for copy in copies:
        copy.start()
    for copy in copies:
        copy.wait()


def per_device(gradients, master, first_moment, second_moment):
    bf16, f32 = jnp.bfloat16, jnp.float32
    anywhere = pl.BlockSpec(memory_space=pl.ANY)
    in_vmem = pl.BlockSpec(memory_space=pltpu.VMEM)
    piece = (4, half, lane)
    dma = pltpu.SemaphoreType.DMA
    params, fresh = pl.pallas_call(
        kernel,
        out_shape=(
            pltpu.VMEM((blocks, width), bf16),
            pltpu.VMEM((3, shard, width), f32),
        ),
        in_specs=[anywhere] * 5,
        out_specs=(in_vmem,) * 2,
        scratch_shapes=[
            pltpu.VMEM((blocks // shard, shard, width), f32),
            pltpu.VMEM((blocks // shard, rows_of, width), f32),
            pltpu.VMEM((rows_of, group), jnp.int32),
            pltpu.VMEM((blocks // 256, 8, width), jnp.int32),
            pltpu.VMEM((group, group), bf16),
            pltpu.VMEM((8, group), f32),
            pltpu.VMEM((8, 8, lane), f32),
            pltpu.VMEM((16, 8, lane), f32),
            pltpu.VMEM((3, shard, width), f32),
            pltpu.VMEM((shard, width), f32),
            pltpu.VMEM((units, 4, 4) + piece, bf16),
            pltpu.VMEM((units, 4, 4) + piece, bf16),
            pltpu.VMEM((units, 4, 4) + piece, bf16),
            pltpu.VMEM((units, 2, 2) + piece, bf16),
            pltpu.VMEM((units, 2, 4) + piece, bf16),
            pltpu.VMEM((units, 4) + piece, bf16),
            pltpu.VMEM((units, 3) + piece, bf16),
            pltpu.VMEM((units,) + piece, bf16),
            pltpu.VMEM((units, 3, half, lane), bf16),
            pltpu.VMEM((units, 64, half, lane), bf16),
            pltpu.VMEM((units, 64, half, lane), bf16),
            dma((chunks,)), dma((1,)), dma((2,)), dma((2,)), dma((3,)), dma((2,)), dma((2,)),
            dma((5,)), dma((units,)), dma((units,)), dma((units,)), dma((units,)), dma((units,)),
            dma((5,)), dma((units,)), dma((units,)), dma((units,)), dma((units,)), dma((units,)),
        ],
        compiler_params=pltpu.CompilerParams(
            collective_id=0, has_side_effects=True, vmem_limit_bytes=50 * 2**20
        ),
        cost_estimate=pl.CostEstimate(flops=2 * 2**32, bytes_accessed=2**25, transcendentals=0),
        name="reduce_step",
    )(gradients, master, first_moment, second_moment, jnp.asarray(sign_words()))
    params, new_master, new_first, new_second = pl.pallas_call(
        write_back,
        out_shape=(
            jax.ShapeDtypeStruct((blocks, width), bf16),
            jax.ShapeDtypeStruct((shard, width), f32),
            jax.ShapeDtypeStruct((shard, width), f32),
            jax.ShapeDtypeStruct((shard, width), f32),
        ),
        in_specs=[in_vmem] * 2,
        out_specs=(anywhere,) * 4,
        scratch_shapes=[dma((1 + 3,))],
        compiler_params=pltpu.CompilerParams(vmem_limit_bytes=2**20),
        name="write_back",
    )(params, fresh)
    return (new_master, new_first, new_second, params)


def solution(mesh):
    in_specs = (
        P(("inner", "outer"), None, None),
        P(("inner", "outer"), None),
        P(("inner", "outer"), None),
        P(("inner", "outer"), None),
    )
    out_specs = (
        P(("inner", "outer"), None),
        P(("inner", "outer"), None),
        P(("inner", "outer"), None),
        P(),
    )
    return jax.shard_map(
        per_device, mesh=mesh, in_specs=in_specs, out_specs=out_specs, check_vma=False
    )
```

```python
import functools
import math

import jax
import jax.numpy as jnp
import numpy as np
from jax import lax
from jax.experimental import pallas as pl
from jax.experimental.pallas import tpu as pltpu
from jax.sharding import PartitionSpec as P

MESH = pl.DeviceIdType.MESH

code_levels = 127.0
beta_one = 0.9
beta_two = 0.95
learn_rate = 0.002
decay_rate = 0.1
adam_epsilon = 1e-08
first_fix = 1.0 - 0.9**10
second_fix = 1.0 - 0.95**10

blocks = 4096
width = 1024
group = 256
shard = 32
half = 16
lane = 128
rows_of = 8
wide = 2 * lane
tiles = width // wide
units = shard // rows_of * tiles
early = tiles
chunk = 512
chunks = blocks // chunk
sub = 512

hash_one = -1640531535
hash_two = ((-2048144777 << 18) & 0xFFFFFFFF) - (1 << 32 if ((-2048144777 << 18) & 0x80000000) else 0)


def wrap(value):
    value &= 0xFFFFFFFF
    return value - (1 << 32) if value & 0x80000000 else value


RS = (0, 0, 7, 14, 22, 29)
AG = (0, 6, 13, 19, 26, 30)


def sign_words():
    at = np.arange(blocks * width, dtype=np.uint32).reshape(blocks, width)
    hashed = (at * np.uint32(hash_one & 0xFFFFFFFF)).view(np.int32)
    hashed = np.bitwise_xor(hashed, np.right_shift(hashed, 15)).view(np.uint32) * np.uint32(-2048144777 & 0xFFFFFFFF)
    bits = ((hashed >> np.uint32(13)) & np.uint32(1)).reshape(blocks // 256, 32, 8, width)
    return (bits << np.arange(32, dtype=np.uint32)[None, :, None, None]).sum(axis=1, dtype=np.uint32).view(np.int32)


def negative(hashed):
    mixed = jnp.bitwise_xor(hashed, jnp.right_shift(hashed, 15))
    return mixed * jnp.int32(hash_two) < 0


def butterfly(parts):
    p0, p1, p2, p3 = parts
    a, b, c, d = p0 + p1, p0 - p1, p2 + p3, p2 - p3
    return a + c, b + d, a - c, b - d


def pick(order, v0, v1, v2):
    return jnp.where(order == 0, v0, jnp.where(order == 1, v1, v2))


def shard_of(axis, v):
    if isinstance(v, int):
        return pick(axis, v, (v % 2) * 4 + (v // 2) * 64, v * 8)
    return pick(axis, v, lax.rem(v, 2) * 4 + lax.div(v, 2) * 64, v * 8)


def kernel(
    grad, master, first, second, words,
    out, fresh,
    rot, twin_rot, base, signs, table, peak, peaks_one, peaks_two, adam_in, total,
    other, core_in, s1, r1, r2, t1, r3, t2, r4, gath, gath_other,
    grad_sem, sign_sem, twin_send, twin_recv, adam_sem, peak_send, peak_recv,
    rs_send, rs_core, rs_one, rs_two, rs_three, rs_four,
    ag_send, ag_one, ag_two, ag_near, ag_far, ag_core,
):
    inner, outer = lax.axis_index("inner"), lax.axis_index("outer")
    core = lax.rem(inner, 2)
    x = lax.rem(outer, 4)
    y = lax.div(inner, 2) * 2 + lax.rem(lax.div(outer, 4), 2)
    z = lax.div(outer, 8)

    def device(xx, yy, zz, cc):
        return (lax.div(yy, 2) * 2 + cc, zz * 8 + lax.rem(yy, 2) * 4 + xx)

    def step(v, d):
        return lax.rem(v + d, 4)

    near = {}
    for d in (1, 2, 3):
        near[0, d] = device(step(x, d), y, z, core)
        near[1, d] = device(x, step(y, d), z, core)
        near[2, d] = device(x, y, step(z, d), core)
    twin = device(x, y, z, 1 - core)

    def along(axis, d):
        return tuple(pick(axis, near[0, d][n], near[1, d][n], near[2, d][n]) for n in (0, 1))

    def remote(src, dst, send, recv, target):
        return pltpu.make_async_remote_copy(
            src_ref=src, dst_ref=dst, send_sem=send, recv_sem=recv, device_id=target, device_id_type=MESH
        )

    def drain(ref, sem):
        pltpu.make_async_copy(ref, ref, sem).wait()

    barrier = pltpu.get_barrier_semaphore()
    column = [device(x, y, step(z, d), c) for d in range(4) for c in (core, 1 - core)][1:]
    plane = [device(step(x, d), step(y, e), z, core) for d in range(4) for e in range(4)][1:]
    partners = column + plane
    for partner in partners:
        pl.semaphore_signal(barrier, inc=1, device_id=partner, device_id_type=MESH)

    def grad_copy(i):
        rows = pl.ds(pl.multiple_of(i * chunk, chunk), chunk)
        return pltpu.make_async_copy(grad.at[0, rows], out.at[rows], grad_sem.at[i])

    def start_grad(i, carry):
        grad_copy(i).start()
        return carry

    sign_copy = pltpu.make_async_copy(words, signs, sign_sem.at[0])
    sign_copy.start()
    lax.fori_loop(0, chunks, start_grad, 0)
    adam_copies = [
        pltpu.make_async_copy(ref, adam_in.at[n], adam_sem.at[n]) for n, ref in enumerate((master, first, second))
    ]
    for copy in adam_copies:
        copy.start()

    rows_i = lax.broadcasted_iota(jnp.int32, (group, group), 0)
    cols_i = lax.broadcasted_iota(jnp.int32, (group, group), 1)
    common = jnp.bitwise_and(rows_i, cols_i)
    for shift in (4, 2, 1):
        common = jnp.bitwise_xor(common, jnp.right_shift(common, shift))
    parity = jnp.bitwise_and(common, 1)
    table[...] = ((1 - 2 * parity).astype(jnp.float32) / math.sqrt(width)).astype(jnp.bfloat16)
    base[...] = (
        lax.broadcasted_iota(jnp.int32, (rows_of, group), 0) * jnp.int32(wrap(width * hash_one))
        + lax.broadcasted_iota(jnp.int32, (rows_of, group), 1) * jnp.int32(hash_one)
    )
    peak[...] = jnp.zeros_like(peak)

    sign_copy.wait()

    def rotate(i, carry):
        grad_copy(i).wait()
        rows = pl.ds(pl.multiple_of(i * sub, sub), sub)
        pieces = []
        for g in range(width // group):
            held = [signs[i * (sub // 256) + n, :, g * group : (g + 1) * group] for n in range(sub // 256)]
            shifted = [jnp.left_shift(word, 31 - r) for word in held for r in range(32)]
            sign = jnp.where(jnp.concatenate(shifted, axis=0) < 0, -1.0, 1.0).astype(jnp.bfloat16)
            flipped = out[rows, g * group : (g + 1) * group] * sign
            pieces.append(flipped)
        turned = jnp.dot(jnp.concatenate(pieces, axis=0), table[...], preferred_element_type=jnp.float32)
        pieces = [turned[g * sub : (g + 1) * sub] for g in range(width // group)]
        top = peak[...]
        for g, piece in enumerate(butterfly(pieces)):
            held = pl.ds(pl.multiple_of(i * (sub // shard), sub // shard), sub // shard)
            rot[held, :, g * group : (g + 1) * group] = piece.reshape(sub // shard, shard, group)
            top = jnp.maximum(top, jnp.max(jnp.abs(piece).reshape(sub // 8, 8, group), axis=0))
        peak[...] = top
        return carry

    lax.fori_loop(0, blocks // sub, rotate, 0)

    pl.semaphore_wait(barrier, len(partners))
    best = jnp.max(jnp.maximum(peak[:, :lane], peak[:, lane:]), axis=0, keepdims=True)
    twin_copies = []
    for n in range(2):
        span = pl.ds(pl.multiple_of(n * 64 + (1 - core) * 32, 32), 32)
        twin_copies.append(
            remote(rot.at[span, pl.ds(0, rows_of)], twin_rot.at[span], twin_send.at[n], twin_recv.at[n], twin)
        )
    for n, (stage, box) in enumerate(((column, peaks_one), (plane, peaks_two))):
        box[0, :1] = best
        for k, target in enumerate(stage):
            remote(box.at[0, :1], box.at[1 + k, :1], peak_send.at[n], peak_recv.at[n], target).start()
        if n == 0:
            for copy in twin_copies:
                copy.start()
        arrived = box.at[pl.ds(1, len(stage)), :1]
        drain(arrived, peak_recv.at[n])
        for k in range(len(stage)):
            best = jnp.maximum(best, box[1 + k, :1])
    scale = jnp.max(best)
    ratio = code_levels / (scale + 1e-06)
    decode = (scale + 1e-06) / (code_levels * 128)

    def fold(value):
        return jnp.concatenate([value[:, :lane], value[:, lane:]], axis=0)

    def quantise(owned, row, column):
        value = rot[owned, pl.ds(row, rows_of), pl.ds(column, wide)]
        return fold(jnp.floor(value * ratio + 0.5))

    def quantise_twin(owned, column):
        value = twin_rot[owned, :, pl.ds(column, wide)]
        return fold(jnp.floor(value * ratio + 0.5))

    def place(u, owner):
        order = lax.rem(u + owner, 3)
        first_row = owner * 1024 + lax.div(u, tiles) * rows_of
        return order, first_row, pl.multiple_of(lax.rem(u, tiles) * wide, wide)

    def axes_of(order):
        a, b, c = order, lax.rem(order + 1, 3), lax.rem(order + 2, 3)
        return a, b, c, pick(a, x, y, z), pick(b, x, y, z), pick(c, x, y, z)

    def each_tile(order, first, work):
        a, b, c = order, lax.rem(order + 1, 3), lax.rem(order + 2, 3)
        in_b = [shard_of(b, j) for j in range(4)]
        in_c = [shard_of(c, k) for k in range(4)]

        def body(i, carry):
            start = first + shard_of(a, i)
            for j in range(4):
                for k in range(4):
                    work(i, j, k, start + in_b[j] + in_c[k])
            return carry

        lax.fori_loop(0, 4, body, 0)

    def row_in(u):
        return pl.multiple_of(lax.div(u, tiles) * rows_of, rows_of)

    def rs0(u):
        order, _, column = place(u, 1 - core)
        row = row_in(u)

        def work(i, j, k, owned):
            other[u, i, j, k] = quantise(owned, row, column).astype(jnp.bfloat16)

        each_tile(order, 32 * (1 - core), work)
        remote(other.at[u], core_in.at[u], rs_send.at[0], rs_core.at[u], twin).start()

    def rs1_early(u):
        order, _, column = place(u, core)
        row = row_in(u)

        def work(i, j, k, owned):
            s1[u, i, j, k] = (quantise(owned, row, column) + quantise_twin(owned, column)).astype(jnp.bfloat16)

        each_tile(order, 32 * core, work)
        send_far(u, order)

    def rs1(u):
        order, _, column = place(u, core)
        row = row_in(u)
        drain(core_in.at[u], rs_core.at[u])

        def work(i, j, k, owned):
            mine = quantise(owned, row, column)
            s1[u, i, j, k] = (mine + core_in[u, i, j, k].astype(jnp.float32)).astype(jnp.bfloat16)

        each_tile(order, 32 * core, work)
        send_far(u, order)

    def send_far(u, order):
        a, _, _, pa, _, _ = axes_of(order)
        up, down = along(a, 1), along(a, 3)
        far = step(pa, 2)
        lo, hi = pl.ds(0, 2), pl.ds(2, 2)
        remote(s1.at[u, far, lo], r1.at[u, 0], rs_send.at[1], rs_one.at[u], up).start()
        remote(s1.at[u, far, hi], r1.at[u, 1], rs_send.at[1], rs_one.at[u], down).start()

    def rs2(u):
        order, _, _ = place(u, core)
        a, _, _, pa, _, _ = axes_of(order)
        pu, pd = step(pa, 1), step(pa, 3)
        lo, hi = pl.ds(0, 2), pl.ds(2, 2)
        drain(r1.at[u], rs_one.at[u])
        s1[u, pu, lo] += r1[u, 0]
        s1[u, pd, hi] += r1[u, 1]
        remote(s1.at[u, pu], r2.at[u, 0], rs_send.at[2], rs_two.at[u], along(a, 1)).start()
        remote(s1.at[u, pd], r2.at[u, 1], rs_send.at[2], rs_two.at[u], along(a, 3)).start()

    def rs3(u):
        order, _, _ = place(u, core)
        _, b, _, pa, pb, _ = axes_of(order)
        drain(r2.at[u], rs_two.at[u])
        f32 = jnp.float32
        t1[u] = (s1[u, pa].astype(f32) + r2[u, 0].astype(f32) + r2[u, 1].astype(f32)).astype(jnp.bfloat16)
        for n, d in enumerate((1, 3, 2)):
            remote(t1.at[u, step(pb, d)], r3.at[u, n], rs_send.at[3], rs_three.at[u], along(b, d)).start()

    def rs4(u):
        order, _, _ = place(u, core)
        _, _, c, _, pb, pc = axes_of(order)
        drain(r3.at[u], rs_three.at[u])
        f32 = jnp.float32
        t2[u] = (
            t1[u, pb].astype(f32) + r3[u, 0].astype(f32) + r3[u, 1].astype(f32) + r3[u, 2].astype(f32)
        ).astype(jnp.bfloat16)
        for n, d in enumerate((1, 3, 2)):
            remote(t2.at[u, step(pc, d)], r4.at[u, n], rs_send.at[4], rs_four.at[u], along(c, d)).start()

    def rs5(u):
        order, _, column = place(u, core)
        pc = axes_of(order)[5]
        drain(r4.at[u], rs_four.at[u])
        f32 = jnp.float32
        value = t2[u, pc].astype(f32) + r4[u, 0].astype(f32) + r4[u, 1].astype(f32) + r4[u, 2].astype(f32)
        rows = pl.ds(pl.multiple_of(lax.div(u, tiles) * rows_of, rows_of), rows_of)
        total[rows, pl.ds(column, lane)] = value[:rows_of]
        total[rows, pl.ds(column + lane, lane)] = value[rows_of:]

        @pl.when(lax.rem(u, tiles) == tiles - 1)
        def _():
            update(lax.div(u, tiles))

    owner = inner * 32 + outer

    def update(h):
        rows = pl.ds(pl.multiple_of(h * rows_of, rows_of), rows_of)
        value = jnp.concatenate([total[rows, g * group : (g + 1) * group] for g in range(width // group)], axis=0)
        high = jnp.floor(value * (1.0 / 128.0) + 0.5)
        stacked = jnp.concatenate([high, value - high * 128.0], axis=0).astype(jnp.bfloat16)
        product = jnp.dot(stacked, table[...], preferred_element_type=jnp.float32)
        product = product[: 4 * rows_of] * 128.0 + product[4 * rows_of :]
        parts = [product[g * rows_of : (g + 1) * rows_of] for g in range(width // group)]
        for g, turned in enumerate(butterfly(parts)):
            columns = slice(g * group, (g + 1) * group)
            offset = (owner * shard + h * rows_of) * jnp.int32(wrap(width * hash_one)) + jnp.int32(wrap(g * group * hash_one))
            mean = turned * decode
            mean = jnp.where(negative(base[...] + offset), -mean, mean)
            one = beta_one * adam_in[1, rows, columns] + (1.0 - beta_one) * mean
            two = beta_two * adam_in[2, rows, columns] + (1.0 - beta_two) * mean * mean
            old = adam_in[0, rows, columns]
            size = one / first_fix / (jnp.sqrt(two / second_fix) + adam_epsilon)
            new = old - learn_rate * (size + decay_rate * old)
            fresh[1, rows, columns] = one
            fresh[2, rows, columns] = two
            fresh[0, rows, columns] = new
            u = h * tiles + g
            order, _, _ = place(u, core)
            _, _, c, pa, pb, pc = axes_of(order)
            mine = pa * 16 + pb * 4 + pc
            gath[u, mine] = fold(new).astype(jnp.bfloat16)
            for d in (1, 3, 2):
                remote(gath.at[u, mine], gath.at[u, mine], ag_send.at[0], ag_one.at[u], along(c, d)).start()

    def ag1(u):
        order, _, _ = place(u, core)
        _, b, _, pa, pb, _ = axes_of(order)
        drain(r4.at[u], ag_one.at[u])
        row = gath.at[u, pl.ds(pa * 16 + pb * 4, 4)]
        for d in (1, 3, 2):
            remote(row, row, ag_send.at[1], ag_two.at[u], along(b, d)).start()

    def ag2(u):
        order, _, _ = place(u, core)
        a, _, _, pa, _, _ = axes_of(order)
        drain(r3.at[u], ag_two.at[u])
        up, down = along(a, 1), along(a, 3)
        lo, hi = gath.at[u, pl.ds(pa * 16, 8)], gath.at[u, pl.ds(pa * 16 + 8, 8)]
        remote(lo, lo, ag_send.at[2], ag_near.at[u], up).start()
        remote(hi, hi, ag_send.at[2], ag_near.at[u], down).start()

    def ag3(u):
        order, _, _ = place(u, core)
        a, _, _, pa, _, _ = axes_of(order)
        drain(r1.at[u], ag_near.at[u])
        lo, hi = gath.at[u, pl.ds(step(pa, 3) * 16, 8)], gath.at[u, pl.ds(step(pa, 1) * 16 + 8, 8)]
        up, down = along(a, 1), along(a, 3)
        remote(lo, lo, ag_send.at[3], ag_far.at[u], up).start()
        remote(hi, hi, ag_send.at[3], ag_far.at[u], down).start()
        lo, hi = gath.at[u, pl.ds(pa * 16, 8)], gath.at[u, pl.ds(pa * 16 + 8, 8)]
        remote(hi, hi, ag_send.at[3], ag_far.at[u], up).start()
        remote(lo, lo, ag_send.at[3], ag_far.at[u], down).start()

    def strides(order):
        return pick(order, 16, 1, 4), pick(order, 4, 16, 1), pick(order, 1, 4, 16)

    def lay_out(u, source, from_core):
        above = u - tiles
        order, first_row, column = place(u, from_core)
        first_row = first_row - rows_of
        su, sa = strides(order), strides(place(above, from_core)[0])

        def body(yy, carry):
            row = first_row + shard_of(1, yy) * shard
            view = out.at[pl.ds(pl.multiple_of(row, half), 880), pl.ds(column, wide)]
            at_u, at_a = yy * su[1], yy * sa[1]
            for zz in range(4):
                for xx in range(4):
                    low = source[u, at_u + xx * su[0] + zz * su[2]].astype(jnp.float32)
                    top = source[above, at_a + xx * sa[0] + zz * sa[2]].astype(jnp.float32)
                    first = xx * shard + zz * 256
                    for n in range(2):
                        part = slice(n * rows_of, (n + 1) * rows_of)
                        both = jnp.concatenate([top[part], low[part]], axis=0)
                        view[first : first + half, n * lane : (n + 1) * lane] = both.astype(jnp.bfloat16)
            return carry

        lax.fori_loop(0, 4, body, 0)

    def is_lower(u):
        return lax.rem(lax.div(u, tiles), 2) == 1

    def ag4(u):
        drain(r2.at[u], ag_far.at[u])
        remote(gath.at[u], gath_other.at[u], ag_send.at[4], ag_core.at[u], twin).start()

        @pl.when(is_lower(u))
        def _():
            lay_out(u, gath, core)

    def ag5(u):
        drain(gath_other.at[u], ag_core.at[u])

        @pl.when(is_lower(u))
        def _():
            lay_out(u, gath_other, 1 - core)

    for copy in adam_copies:
        copy.wait()
    lead = tiles - 1 + RS[5]
    plan = [(rs1, RS[1], early), (rs2, RS[2], 0), (rs3, RS[3], 0), (rs4, RS[4], 0), (rs5, RS[5], 0)]
    plan += [(work, lead + AG[n + 1], 0) for n, work in enumerate((ag1, ag2, ag3, ag4, ag5))]
    for copy in twin_copies:
        copy.wait_recv()

    def repeat(work, begin, end):
        def body(u, carry):
            work(u)
            return carry

        lax.fori_loop(begin, end, body, 0)

    repeat(rs1_early, 0, early)
    repeat(rs0, early, units)

    marks = sorted({delay + first for _, delay, first in plan} | {delay + units for _, delay, _ in plan})
    for begin, end in zip(marks, marks[1:]):
        running = [(work, delay) for work, delay, first in plan if delay + first <= begin and end <= delay + units]

        def tick(t, running=running):
            for work, delay in running:
                work(t - delay)

        repeat(tick, begin, end)

    for copy in twin_copies:
        copy.wait_send()
    for n, box in enumerate((peaks_one, peaks_two)):
        drain(box.at[pl.ds(1, (7, 15)[n]), :1], peak_send.at[n])
    drain(other.at[pl.ds(early, units - early)], rs_send.at[0])
    drain(r1, rs_send.at[1])
    drain(r2, rs_send.at[2])
    drain(r3, rs_send.at[3])
    drain(r4, rs_send.at[4])
    drain(r4, ag_send.at[0])
    drain(r3, ag_send.at[1])
    drain(r1, ag_send.at[2])
    drain(r2, ag_send.at[3])
    drain(gath, ag_send.at[4])


def write_back(params, fresh, out, new_master, new_first, new_second, sems):
    parts = 1
    span = blocks // parts
    copies = [pltpu.make_async_copy(fresh.at[n], ref, sems.at[n]) for n, ref in enumerate((new_master, new_first, new_second))]
    for n in range(parts):
        rows = pl.ds(n * span, span)
        copies.append(pltpu.make_async_copy(params.at[rows], out.at[rows], sems.at[3 + n]))
    for copy in copies:
        copy.start()
    for copy in copies:
        copy.wait()


def per_device(gradients, master, first_moment, second_moment):
    bf16, f32 = jnp.bfloat16, jnp.float32
    anywhere = pl.BlockSpec(memory_space=pl.ANY)
    in_vmem = pl.BlockSpec(memory_space=pltpu.VMEM)
    piece = (4, half, lane)
    dma = pltpu.SemaphoreType.DMA
    params, fresh = pl.pallas_call(
        kernel,
        out_shape=(
            pltpu.VMEM((blocks, width), bf16),
            pltpu.VMEM((3, shard, width), f32),
        ),
        in_specs=[anywhere] * 5,
        out_specs=(in_vmem,) * 2,
        scratch_shapes=[
            pltpu.VMEM((blocks // shard, shard, width), f32),
            pltpu.VMEM((blocks // shard, rows_of, width), f32),
            pltpu.VMEM((rows_of, group), jnp.int32),
            pltpu.VMEM((blocks // 256, 8, width), jnp.int32),
            pltpu.VMEM((group, group), bf16),
            pltpu.VMEM((8, group), f32),
            pltpu.VMEM((8, 8, lane), f32),
            pltpu.VMEM((16, 8, lane), f32),
            pltpu.VMEM((3, shard, width), f32),
            pltpu.VMEM((shard, width), f32),
            pltpu.VMEM((units, 4, 4) + piece, bf16),
            pltpu.VMEM((units, 4, 4) + piece, bf16),
            pltpu.VMEM((units, 4, 4) + piece, bf16),
            pltpu.VMEM((units, 2, 2) + piece, bf16),
            pltpu.VMEM((units, 2, 4) + piece, bf16),
            pltpu.VMEM((units, 4) + piece, bf16),
            pltpu.VMEM((units, 3) + piece, bf16),
            pltpu.VMEM((units,) + piece, bf16),
            pltpu.VMEM((units, 3, half, lane), bf16),
            pltpu.VMEM((units, 64, half, lane), bf16),
            pltpu.VMEM((units, 64, half, lane), bf16),
            dma((chunks,)), dma((1,)), dma((2,)), dma((2,)), dma((3,)), dma((2,)), dma((2,)),
            dma((5,)), dma((units,)), dma((units,)), dma((units,)), dma((units,)), dma((units,)),
            dma((5,)), dma((units,)), dma((units,)), dma((units,)), dma((units,)), dma((units,)),
        ],
        compiler_params=pltpu.CompilerParams(
            collective_id=0, has_side_effects=True, vmem_limit_bytes=50 * 2**20
        ),
        cost_estimate=pl.CostEstimate(flops=2 * 2**32, bytes_accessed=2**25, transcendentals=0),
        name="reduce_step",
    )(gradients, master, first_moment, second_moment, jnp.asarray(sign_words()))
    params, new_master, new_first, new_second = pl.pallas_call(
        write_back,
        out_shape=(
            jax.ShapeDtypeStruct((blocks, width), bf16),
            jax.ShapeDtypeStruct((shard, width), f32),
            jax.ShapeDtypeStruct((shard, width), f32),
            jax.ShapeDtypeStruct((shard, width), f32),
        ),
        in_specs=[in_vmem] * 2,
        out_specs=(anywhere,) * 4,
        scratch_shapes=[dma((1 + 3,))],
        compiler_params=pltpu.CompilerParams(vmem_limit_bytes=2**20),
        name="write_back",
    )(params, fresh)
    return (new_master, new_first, new_second, params)


def solution(mesh):
    in_specs = (
        P(("inner", "outer"), None, None),
        P(("inner", "outer"), None),
        P(("inner", "outer"), None),
        P(("inner", "outer"), None),
    )
    out_specs = (
        P(("inner", "outer"), None),
        P(("inner", "outer"), None),
        P(("inner", "outer"), None),
        P(),
    )
    return jax.shard_map(
        per_device, mesh=mesh, in_specs=in_specs, out_specs=out_specs, check_vma=False
    )
```

```python
import functools
import math

import jax
import jax.numpy as jnp
import numpy as np
from jax import lax
from jax.experimental import pallas as pl
from jax.experimental.pallas import tpu as pltpu
from jax.sharding import PartitionSpec as P

MESH = pl.DeviceIdType.MESH

code_levels = 127.0
beta_one = 0.9
beta_two = 0.95
learn_rate = 0.002
decay_rate = 0.1
adam_epsilon = 1e-08
first_fix = 1.0 - 0.9**10
second_fix = 1.0 - 0.95**10

blocks = 4096
width = 1024
group = 256
shard = 32
half = 16
lane = 128
rows_of = 8
wide = 2 * lane
tiles = width // wide
units = shard // rows_of * tiles
early = tiles
chunk = 512
chunks = blocks // chunk
sub = 512

hash_one = -1640531535
hash_two = ((-2048144777 << 18) & 0xFFFFFFFF) - (1 << 32 if ((-2048144777 << 18) & 0x80000000) else 0)


def wrap(value):
    value &= 0xFFFFFFFF
    return value - (1 << 32) if value & 0x80000000 else value


RS = (0, 0, 7, 14, 22, 29)
AG = (0, 6, 13, 19, 26, 30)


def sign_words():
    at = np.arange(blocks * width, dtype=np.uint32).reshape(blocks, width)
    hashed = (at * np.uint32(hash_one & 0xFFFFFFFF)).view(np.int32)
    hashed = np.bitwise_xor(hashed, np.right_shift(hashed, 15)).view(np.uint32) * np.uint32(-2048144777 & 0xFFFFFFFF)
    bits = ((hashed >> np.uint32(13)) & np.uint32(1)).reshape(blocks // 256, 32, 8, width)
    return (bits << np.arange(32, dtype=np.uint32)[None, :, None, None]).sum(axis=1, dtype=np.uint32).view(np.int32)


def negative(hashed):
    mixed = jnp.bitwise_xor(hashed, jnp.right_shift(hashed, 15))
    return mixed * jnp.int32(hash_two) < 0


def butterfly(parts):
    p0, p1, p2, p3 = parts
    a, b, c, d = p0 + p1, p0 - p1, p2 + p3, p2 - p3
    return a + c, b + d, a - c, b - d


def pick(order, v0, v1, v2):
    return jnp.where(order == 0, v0, jnp.where(order == 1, v1, v2))


def shard_of(axis, v):
    if isinstance(v, int):
        return pick(axis, v, (v % 2) * 4 + (v // 2) * 64, v * 8)
    return pick(axis, v, lax.rem(v, 2) * 4 + lax.div(v, 2) * 64, v * 8)


def kernel(
    grad, master, first, second, words,
    out, fresh,
    rot, twin_rot, base, signs, table, peak, peaks_one, peaks_two, adam_in, total,
    other, core_in, s1, r1, r2, t1, r3, t2, r4, gath, gath_other,
    grad_sem, sign_sem, twin_send, twin_recv, adam_sem, peak_send, peak_recv,
    rs_send, rs_core, rs_one, rs_two, rs_three, rs_four,
    ag_send, ag_one, ag_two, ag_near, ag_far, ag_core,
):
    inner, outer = lax.axis_index("inner"), lax.axis_index("outer")
    core = lax.rem(inner, 2)
    x = lax.rem(outer, 4)
    y = lax.div(inner, 2) * 2 + lax.rem(lax.div(outer, 4), 2)
    z = lax.div(outer, 8)

    def device(xx, yy, zz, cc):
        return (lax.div(yy, 2) * 2 + cc, zz * 8 + lax.rem(yy, 2) * 4 + xx)

    def step(v, d):
        return lax.rem(v + d, 4)

    near = {}
    for d in (1, 2, 3):
        near[0, d] = device(step(x, d), y, z, core)
        near[1, d] = device(x, step(y, d), z, core)
        near[2, d] = device(x, y, step(z, d), core)
    twin = device(x, y, z, 1 - core)

    def along(axis, d):
        return tuple(pick(axis, near[0, d][n], near[1, d][n], near[2, d][n]) for n in (0, 1))

    def remote(src, dst, send, recv, target):
        return pltpu.make_async_remote_copy(
            src_ref=src, dst_ref=dst, send_sem=send, recv_sem=recv, device_id=target, device_id_type=MESH
        )

    def drain(ref, sem):
        pltpu.make_async_copy(ref, ref, sem).wait()

    barrier = pltpu.get_barrier_semaphore()
    column = [device(x, y, step(z, d), c) for d in range(4) for c in (core, 1 - core)][1:]
    plane = [device(step(x, d), step(y, e), z, core) for d in range(4) for e in range(4)][1:]
    partners = column + plane
    for partner in partners:
        pl.semaphore_signal(barrier, inc=1, device_id=partner, device_id_type=MESH)

    def grad_copy(i):
        rows = pl.ds(pl.multiple_of(i * chunk, chunk), chunk)
        return pltpu.make_async_copy(grad.at[0, rows], out.at[rows], grad_sem.at[i])

    def start_grad(i, carry):
        grad_copy(i).start()
        return carry

    sign_copy = pltpu.make_async_copy(words, signs, sign_sem.at[0])
    sign_copy.start()
    lax.fori_loop(0, chunks, start_grad, 0)
    adam_copies = [
        pltpu.make_async_copy(ref, adam_in.at[n], adam_sem.at[n]) for n, ref in enumerate((master, first, second))
    ]
    for copy in adam_copies:
        copy.start()

    rows_i = lax.broadcasted_iota(jnp.int32, (group, group), 0)
    cols_i = lax.broadcasted_iota(jnp.int32, (group, group), 1)
    common = jnp.bitwise_and(rows_i, cols_i)
    for shift in (4, 2, 1):
        common = jnp.bitwise_xor(common, jnp.right_shift(common, shift))
    parity = jnp.bitwise_and(common, 1)
    table[...] = ((1 - 2 * parity).astype(jnp.float32) / math.sqrt(width)).astype(jnp.bfloat16)
    base[...] = (
        lax.broadcasted_iota(jnp.int32, (rows_of, group), 0) * jnp.int32(wrap(width * hash_one))
        + lax.broadcasted_iota(jnp.int32, (rows_of, group), 1) * jnp.int32(hash_one)
    )
    peak[...] = jnp.zeros_like(peak)

    sign_copy.wait()

    def rotate(i, carry):
        grad_copy(i).wait()
        rows = pl.ds(pl.multiple_of(i * sub, sub), sub)
        pieces = []
        for g in range(width // group):
            held = [signs[i * (sub // 256) + n, :, g * group : (g + 1) * group] for n in range(sub // 256)]
            shifted = [jnp.left_shift(word, 31 - r) for word in held for r in range(32)]
            sign = jnp.where(jnp.concatenate(shifted, axis=0) < 0, -1.0, 1.0).astype(jnp.bfloat16)
            flipped = out[rows, g * group : (g + 1) * group] * sign
            pieces.append(flipped)
        turned = jnp.dot(jnp.concatenate(pieces, axis=0), table[...], preferred_element_type=jnp.float32)
        pieces = [turned[g * sub : (g + 1) * sub] for g in range(width // group)]
        top = peak[...]
        for g, piece in enumerate(butterfly(pieces)):
            held = pl.ds(pl.multiple_of(i * (sub // shard), sub // shard), sub // shard)
            rot[held, :, g * group : (g + 1) * group] = piece.reshape(sub // shard, shard, group)
            top = jnp.maximum(top, jnp.max(jnp.abs(piece).reshape(sub // 8, 8, group), axis=0))
        peak[...] = top
        return carry

    lax.fori_loop(0, blocks // sub, rotate, 0)

    pl.semaphore_wait(barrier, len(partners))
    best = jnp.max(jnp.maximum(peak[:, :lane], peak[:, lane:]), axis=0, keepdims=True)
    twin_copies = []
    for n in range(2):
        span = pl.ds(pl.multiple_of(n * 64 + (1 - core) * 32, 32), 32)
        twin_copies.append(
            remote(rot.at[span, pl.ds(0, rows_of)], twin_rot.at[span], twin_send.at[n], twin_recv.at[n], twin)
        )
    for n, (stage, box) in enumerate(((column, peaks_one), (plane, peaks_two))):
        box[0, :1] = best
        for k, target in enumerate(stage):
            remote(box.at[0, :1], box.at[1 + k, :1], peak_send.at[n], peak_recv.at[n], target).start()
        if n == 0:
            for copy in twin_copies:
                copy.start()
        arrived = box.at[pl.ds(1, len(stage)), :1]
        drain(arrived, peak_recv.at[n])
        for k in range(len(stage)):
            best = jnp.maximum(best, box[1 + k, :1])
    scale = jnp.max(best)
    ratio = code_levels / (scale + 1e-06)
    decode = (scale + 1e-06) / (code_levels * 128)

    def fold(value):
        return jnp.concatenate([value[:, :lane], value[:, lane:]], axis=0)

    def quantise(owned, row, column):
        value = rot[owned, pl.ds(row, rows_of), pl.ds(column, wide)]
        return fold(jnp.floor(value * ratio + 0.5))

    def quantise_twin(owned, column):
        value = twin_rot[owned, :, pl.ds(column, wide)]
        return fold(jnp.floor(value * ratio + 0.5))

    def place(u, owner):
        order = lax.rem(u + owner, 3)
        first_row = owner * 1024 + lax.div(u, tiles) * rows_of
        return order, first_row, pl.multiple_of(lax.rem(u, tiles) * wide, wide)

    def axes_of(order):
        a, b, c = order, lax.rem(order + 1, 3), lax.rem(order + 2, 3)
        return a, b, c, pick(a, x, y, z), pick(b, x, y, z), pick(c, x, y, z)

    def each_tile(order, first, work):
        a, b, c = order, lax.rem(order + 1, 3), lax.rem(order + 2, 3)
        in_b = [shard_of(b, j) for j in range(4)]
        in_c = [shard_of(c, k) for k in range(4)]

        def body(i, carry):
            start = first + shard_of(a, i)
            for j in range(4):
                for k in range(4):
                    work(i, j, k, start + in_b[j] + in_c[k])
            return carry

        lax.fori_loop(0, 4, body, 0)

    def row_in(u):
        return pl.multiple_of(lax.div(u, tiles) * rows_of, rows_of)

    def rs0(u):
        order, _, column = place(u, 1 - core)
        row = row_in(u)

        def work(i, j, k, owned):
            other[u, i, j, k] = quantise(owned, row, column).astype(jnp.bfloat16)

        each_tile(order, 32 * (1 - core), work)
        remote(other.at[u], core_in.at[u], rs_send.at[0], rs_core.at[u], twin).start()

    def rs1_early(u):
        order, _, column = place(u, core)
        row = row_in(u)

        def work(i, j, k, owned):
            s1[u, i, j, k] = (quantise(owned, row, column) + quantise_twin(owned, column)).astype(jnp.bfloat16)

        each_tile(order, 32 * core, work)
        send_far(u, order)

    def rs1(u):
        order, _, column = place(u, core)
        row = row_in(u)
        drain(core_in.at[u], rs_core.at[u])

        def work(i, j, k, owned):
            mine = quantise(owned, row, column)
            s1[u, i, j, k] = (mine + core_in[u, i, j, k].astype(jnp.float32)).astype(jnp.bfloat16)

        each_tile(order, 32 * core, work)
        send_far(u, order)

    def send_far(u, order):
        a, _, _, pa, _, _ = axes_of(order)
        up, down = along(a, 1), along(a, 3)
        far = step(pa, 2)
        lo, hi = pl.ds(0, 2), pl.ds(2, 2)
        remote(s1.at[u, far, lo], r1.at[u, 0], rs_send.at[1], rs_one.at[u], up).start()
        remote(s1.at[u, far, hi], r1.at[u, 1], rs_send.at[1], rs_one.at[u], down).start()

    def rs2(u):
        order, _, _ = place(u, core)
        a, _, _, pa, _, _ = axes_of(order)
        pu, pd = step(pa, 1), step(pa, 3)
        lo, hi = pl.ds(0, 2), pl.ds(2, 2)
        drain(r1.at[u], rs_one.at[u])
        s1[u, pu, lo] += r1[u, 0]
        s1[u, pd, hi] += r1[u, 1]
        remote(s1.at[u, pu], r2.at[u, 0], rs_send.at[2], rs_two.at[u], along(a, 1)).start()
        remote(s1.at[u, pd], r2.at[u, 1], rs_send.at[2], rs_two.at[u], along(a, 3)).start()

    def rs3(u):
        order, _, _ = place(u, core)
        _, b, _, pa, pb, _ = axes_of(order)
        drain(r2.at[u], rs_two.at[u])
        f32 = jnp.float32
        t1[u] = (s1[u, pa].astype(f32) + r2[u, 0].astype(f32) + r2[u, 1].astype(f32)).astype(jnp.bfloat16)
        for n, d in enumerate((1, 3, 2)):
            remote(t1.at[u, step(pb, d)], r3.at[u, n], rs_send.at[3], rs_three.at[u], along(b, d)).start()

    def rs4(u):
        order, _, _ = place(u, core)
        _, _, c, _, pb, pc = axes_of(order)
        drain(r3.at[u], rs_three.at[u])
        f32 = jnp.float32
        t2[u] = (
            t1[u, pb].astype(f32) + r3[u, 0].astype(f32) + r3[u, 1].astype(f32) + r3[u, 2].astype(f32)
        ).astype(jnp.bfloat16)
        for n, d in enumerate((1, 3, 2)):
            remote(t2.at[u, step(pc, d)], r4.at[u, n], rs_send.at[4], rs_four.at[u], along(c, d)).start()

    def rs5(u):
        order, _, column = place(u, core)
        pc = axes_of(order)[5]
        drain(r4.at[u], rs_four.at[u])
        f32 = jnp.float32
        value = t2[u, pc].astype(f32) + r4[u, 0].astype(f32) + r4[u, 1].astype(f32) + r4[u, 2].astype(f32)
        rows = pl.ds(pl.multiple_of(lax.div(u, tiles) * rows_of, rows_of), rows_of)
        total[rows, pl.ds(column, lane)] = value[:rows_of]
        total[rows, pl.ds(column + lane, lane)] = value[rows_of:]

        @pl.when(lax.rem(u, tiles) == tiles - 1)
        def _():
            update(lax.div(u, tiles))

    owner = inner * 32 + outer

    def update(h):
        rows = pl.ds(pl.multiple_of(h * rows_of, rows_of), rows_of)
        value = jnp.concatenate([total[rows, g * group : (g + 1) * group] for g in range(width // group)], axis=0)
        high = jnp.floor(value * (1.0 / 128.0) + 0.5)
        stacked = jnp.concatenate([high, value - high * 128.0], axis=0).astype(jnp.bfloat16)
        product = jnp.dot(stacked, table[...], preferred_element_type=jnp.float32)
        product = product[: 4 * rows_of] * 128.0 + product[4 * rows_of :]
        parts = [product[g * rows_of : (g + 1) * rows_of] for g in range(width // group)]
        for g, turned in enumerate(butterfly(parts)):
            columns = slice(g * group, (g + 1) * group)
            offset = (owner * shard + h * rows_of) * jnp.int32(wrap(width * hash_one)) + jnp.int32(wrap(g * group * hash_one))
            mean = turned * decode
            mean = jnp.where(negative(base[...] + offset), -mean, mean)
            one = beta_one * adam_in[1, rows, columns] + (1.0 - beta_one) * mean
            two = beta_two * adam_in[2, rows, columns] + (1.0 - beta_two) * mean * mean
            old = adam_in[0, rows, columns]
            size = one / first_fix / (jnp.sqrt(two / second_fix) + adam_epsilon)
            new = old - learn_rate * (size + decay_rate * old)
            fresh[1, rows, columns] = one
            fresh[2, rows, columns] = two
            fresh[0, rows, columns] = new
            u = h * tiles + g
            order, _, _ = place(u, core)
            _, _, c, pa, pb, pc = axes_of(order)
            mine = pa * 16 + pb * 4 + pc
            gath[u, mine] = fold(new).astype(jnp.bfloat16)
            for d in (1, 3, 2):
                remote(gath.at[u, mine], gath.at[u, mine], ag_send.at[0], ag_one.at[u], along(c, d)).start()

    def ag1(u):
        order, _, _ = place(u, core)
        _, b, _, pa, pb, _ = axes_of(order)
        drain(r4.at[u], ag_one.at[u])
        row = gath.at[u, pl.ds(pa * 16 + pb * 4, 4)]
        for d in (1, 3, 2):
            remote(row, row, ag_send.at[1], ag_two.at[u], along(b, d)).start()

    def ag2(u):
        order, _, _ = place(u, core)
        a, _, _, pa, _, _ = axes_of(order)
        drain(r3.at[u], ag_two.at[u])
        up, down = along(a, 1), along(a, 3)
        lo, hi = gath.at[u, pl.ds(pa * 16, 8)], gath.at[u, pl.ds(pa * 16 + 8, 8)]
        remote(lo, lo, ag_send.at[2], ag_near.at[u], up).start()
        remote(hi, hi, ag_send.at[2], ag_near.at[u], down).start()

    def ag3(u):
        order, _, _ = place(u, core)
        a, _, _, pa, _, _ = axes_of(order)
        drain(r1.at[u], ag_near.at[u])
        lo, hi = gath.at[u, pl.ds(step(pa, 3) * 16, 8)], gath.at[u, pl.ds(step(pa, 1) * 16 + 8, 8)]
        up, down = along(a, 1), along(a, 3)
        remote(lo, lo, ag_send.at[3], ag_far.at[u], up).start()
        remote(hi, hi, ag_send.at[3], ag_far.at[u], down).start()
        lo, hi = gath.at[u, pl.ds(pa * 16, 8)], gath.at[u, pl.ds(pa * 16 + 8, 8)]
        remote(hi, hi, ag_send.at[3], ag_far.at[u], up).start()
        remote(lo, lo, ag_send.at[3], ag_far.at[u], down).start()

    def strides(order):
        return pick(order, 16, 1, 4), pick(order, 4, 16, 1), pick(order, 1, 4, 16)

    def lay_out(u, source, from_core):
        above = u - tiles
        order, first_row, column = place(u, from_core)
        first_row = first_row - rows_of
        su, sa = strides(order), strides(place(above, from_core)[0])

        def body(yy, carry):
            row = first_row + shard_of(1, yy) * shard
            view = out.at[pl.ds(pl.multiple_of(row, half), 880), pl.ds(column, wide)]
            at_u, at_a = yy * su[1], yy * sa[1]
            for zz in range(4):
                for xx in range(4):
                    low = source[u, at_u + xx * su[0] + zz * su[2]].astype(jnp.float32)
                    top = source[above, at_a + xx * sa[0] + zz * sa[2]].astype(jnp.float32)
                    first = xx * shard + zz * 256
                    for n in range(2):
                        part = slice(n * rows_of, (n + 1) * rows_of)
                        both = jnp.concatenate([top[part], low[part]], axis=0)
                        view[first : first + half, n * lane : (n + 1) * lane] = both.astype(jnp.bfloat16)
            return carry

        lax.fori_loop(0, 4, body, 0, unroll=True)

    def is_lower(u):
        return lax.rem(lax.div(u, tiles), 2) == 1

    def ag4(u):
        drain(r2.at[u], ag_far.at[u])
        remote(gath.at[u], gath_other.at[u], ag_send.at[4], ag_core.at[u], twin).start()

        @pl.when(is_lower(u))
        def _():
            lay_out(u, gath, core)

    def ag5(u):
        drain(gath_other.at[u], ag_core.at[u])

        @pl.when(is_lower(u))
        def _():
            lay_out(u, gath_other, 1 - core)

    for copy in adam_copies:
        copy.wait()
    lead = tiles - 1 + RS[5]
    plan = [(rs1, RS[1], early), (rs2, RS[2], 0), (rs3, RS[3], 0), (rs4, RS[4], 0), (rs5, RS[5], 0)]
    plan += [(work, lead + AG[n + 1], 0) for n, work in enumerate((ag1, ag2, ag3, ag4, ag5))]
    for copy in twin_copies:
        copy.wait_recv()

    def repeat(work, begin, end):
        def body(u, carry):
            work(u)
            return carry

        lax.fori_loop(begin, end, body, 0)

    repeat(rs1_early, 0, early)
    repeat(rs0, early, units)

    marks = sorted({delay + first for _, delay, first in plan} | {delay + units for _, delay, _ in plan})
    for begin, end in zip(marks, marks[1:]):
        running = [(work, delay) for work, delay, first in plan if delay + first <= begin and end <= delay + units]

        def tick(t, running=running):
            for work, delay in running:
                work(t - delay)

        repeat(tick, begin, end)

    for copy in twin_copies:
        copy.wait_send()
    for n, box in enumerate((peaks_one, peaks_two)):
        drain(box.at[pl.ds(1, (7, 15)[n]), :1], peak_send.at[n])
    drain(other.at[pl.ds(early, units - early)], rs_send.at[0])
    drain(r1, rs_send.at[1])
    drain(r2, rs_send.at[2])
    drain(r3, rs_send.at[3])
    drain(r4, rs_send.at[4])
    drain(r4, ag_send.at[0])
    drain(r3, ag_send.at[1])
    drain(r1, ag_send.at[2])
    drain(r2, ag_send.at[3])
    drain(gath, ag_send.at[4])


def write_back(params, fresh, out, new_master, new_first, new_second, sems):
    parts = 1
    span = blocks // parts
    copies = [pltpu.make_async_copy(fresh.at[n], ref, sems.at[n]) for n, ref in enumerate((new_master, new_first, new_second))]
    for n in range(parts):
        rows = pl.ds(n * span, span)
        copies.append(pltpu.make_async_copy(params.at[rows], out.at[rows], sems.at[3 + n]))
    for copy in copies:
        copy.start()
    for copy in copies:
        copy.wait()


def per_device(gradients, master, first_moment, second_moment):
    bf16, f32 = jnp.bfloat16, jnp.float32
    anywhere = pl.BlockSpec(memory_space=pl.ANY)
    in_vmem = pl.BlockSpec(memory_space=pltpu.VMEM)
    piece = (4, half, lane)
    dma = pltpu.SemaphoreType.DMA
    params, fresh = pl.pallas_call(
        kernel,
        out_shape=(
            pltpu.VMEM((blocks, width), bf16),
            pltpu.VMEM((3, shard, width), f32),
        ),
        in_specs=[anywhere] * 5,
        out_specs=(in_vmem,) * 2,
        scratch_shapes=[
            pltpu.VMEM((blocks // shard, shard, width), f32),
            pltpu.VMEM((blocks // shard, rows_of, width), f32),
            pltpu.VMEM((rows_of, group), jnp.int32),
            pltpu.VMEM((blocks // 256, 8, width), jnp.int32),
            pltpu.VMEM((group, group), bf16),
            pltpu.VMEM((8, group), f32),
            pltpu.VMEM((8, 8, lane), f32),
            pltpu.VMEM((16, 8, lane), f32),
            pltpu.VMEM((3, shard, width), f32),
            pltpu.VMEM((shard, width), f32),
            pltpu.VMEM((units, 4, 4) + piece, bf16),
            pltpu.VMEM((units, 4, 4) + piece, bf16),
            pltpu.VMEM((units, 4, 4) + piece, bf16),
            pltpu.VMEM((units, 2, 2) + piece, bf16),
            pltpu.VMEM((units, 2, 4) + piece, bf16),
            pltpu.VMEM((units, 4) + piece, bf16),
            pltpu.VMEM((units, 3) + piece, bf16),
            pltpu.VMEM((units,) + piece, bf16),
            pltpu.VMEM((units, 3, half, lane), bf16),
            pltpu.VMEM((units, 64, half, lane), bf16),
            pltpu.VMEM((units, 64, half, lane), bf16),
            dma((chunks,)), dma((1,)), dma((2,)), dma((2,)), dma((3,)), dma((2,)), dma((2,)),
            dma((5,)), dma((units,)), dma((units,)), dma((units,)), dma((units,)), dma((units,)),
            dma((5,)), dma((units,)), dma((units,)), dma((units,)), dma((units,)), dma((units,)),
        ],
        compiler_params=pltpu.CompilerParams(
            collective_id=0, has_side_effects=True, vmem_limit_bytes=50 * 2**20
        ),
        cost_estimate=pl.CostEstimate(flops=2 * 2**32, bytes_accessed=2**25, transcendentals=0),
        name="reduce_step",
    )(gradients, master, first_moment, second_moment, jnp.asarray(sign_words()))
    params, new_master, new_first, new_second = pl.pallas_call(
        write_back,
        out_shape=(
            jax.ShapeDtypeStruct((blocks, width), bf16),
            jax.ShapeDtypeStruct((shard, width), f32),
            jax.ShapeDtypeStruct((shard, width), f32),
            jax.ShapeDtypeStruct((shard, width), f32),
        ),
        in_specs=[in_vmem] * 2,
        out_specs=(anywhere,) * 4,
        scratch_shapes=[dma((1 + 3,))],
        compiler_params=pltpu.CompilerParams(vmem_limit_bytes=2**20),
        name="write_back",
    )(params, fresh)
    return (new_master, new_first, new_second, params)


def solution(mesh):
    in_specs = (
        P(("inner", "outer"), None, None),
        P(("inner", "outer"), None),
        P(("inner", "outer"), None),
        P(("inner", "outer"), None),
    )
    out_specs = (
        P(("inner", "outer"), None),
        P(("inner", "outer"), None),
        P(("inner", "outer"), None),
        P(),
    )
    return jax.shard_map(
        per_device, mesh=mesh, in_specs=in_specs, out_specs=out_specs, check_vma=False
    )
```
